128 devices in a mesh: space: 16 (over y, z), grp: 8 (over x, core).
Axes of the slice: x: 4, y: 4, z: 4, core: 2. Of those that a mesh axis runs over, the one named last changes fastest.
Arguments:
- rel_vec: float32 [3, 262144], P(None, ('space', 'grp'))
- atom_feat: bfloat16 [32768, 256], P(('space', 'grp')), may hold values from -6 to 6
- centre: int32 [262144], P(('space', 'grp')), may hold values from 0 to 255
- nbr_slot: int32 [262144], P(('space', 'grp')), may hold values from 0 to 1279, as said below
- edge_mask: int32 [262144], P(('space', 'grp')), may hold values from 0 to 1, as said below
- send_rows: int32 [128, 128], P(('space', 'grp')), may hold values from 0 to 255, as said below
- w_radial: float32 [8, 256], replicated, may hold values from -2 to 2
- w_centre: bfloat16 [256, 256], replicated, may hold values from -0.375 to 0.375
- w_nbr: bfloat16 [256, 256], replicated, may hold values from -0.375 to 0.375
- w_env: bfloat16 [256, 64], replicated, may hold values from -0.375 to 0.375
- w_val: bfloat16 [256, 64], replicated, may hold values from -0.375 to 0.375
- w_mix: bfloat16 [256, 256], replicated, may hold values from -0.375 to 0.375
- w_scal: bfloat16 [192, 256], replicated, may hold values from -0.4375 to 0.4375
- w_read: bfloat16 [256, 256], replicated, may hold values from -0.375 to 0.375
- w_out: float32 [256], replicated, may hold values from -0.375 to 0.375
Outputs:
- atom_energy: float32 [32768], P(('space', 'grp'))
- forces: float32 [3, 32768], P(None, ('space', 'grp'))
The draws below stay inside these ranges and needn't reach their ends.
Inputs may be any that keep to these rules, and one draw needn't show every extreme that they name: `nbr_slot`: every row of a device's table, 256 own rows and 1024 received ones, is named by at least one edge of that device. `edge_mask`: within each aligned block of 128 edges the real edges form a leading run; some blocks are empty, and how many differs from device to device. `send_rows`: the 128 atoms of one device's list are distinct.
All inputs are finite; a program needn't handle non-finite values.
Results may differ from the reference program's by a relative error of at most 0.015.
Values may be sent and summed in bfloat16 or wider, within the bound.
A program may use at most 64 MiB of HBM per device.

```python
import math
import jax
import jax.numpy as jnp
from jax import lax

D = 256
C = 64
NB = 8
ATOM_DEV = 256
SLOTS = 128
EDGE_DEV = 2048
ATOMS = 32768
EDGES = 262144
N_SPACE = 16
N_GRP = 8


def draw_rel_vec(key, part):
    key = jax.random.fold_in(key, 5)
    key_len, key_cos, key_phi = jax.random.split(key, 3)
    level = jax.random.uniform(key_len, (EDGES,), jnp.float32)
    length = 0.9 + 3.9 * level
    cosine = jax.random.uniform(key_cos, (EDGES,), jnp.float32, -1.0, 1.0)
    phase = jax.random.uniform(key_phi, (EDGES,), jnp.float32, -math.pi, math.pi)
    sine = jnp.sqrt(jnp.maximum(1.0 - cosine * cosine, 0.0))
    return jnp.stack([length * sine * jnp.cos(phase), length * sine * jnp.sin(phase), length * cosine], axis=0).astype(jnp.float32)


def draw_nbr_slot(key, part):
    key = jax.random.fold_in(key, 7)
    key_perm, key_rest, key_mix = jax.random.split(key, 3)
    devices = N_SPACE * N_GRP
    slot_count = ATOM_DEV + 8 * SLOTS
    firsts = jax.vmap(lambda k: jax.random.permutation(k, slot_count))(jax.random.split(key_perm, devices))
    others = jax.random.randint(key_rest, (devices, EDGE_DEV - slot_count), 0, slot_count)
    joined = jnp.concatenate([firsts.astype(jnp.int32), others.astype(jnp.int32)], axis=1)
    mixed = jax.vmap(lambda k, row: jax.random.permutation(k, row))(jax.random.split(key_mix, devices), joined)
    return mixed.reshape(EDGES).astype(jnp.int32)


def draw_edge_mask(key, part):
    key = jax.random.fold_in(key, 11)
    key_count, key_level, key_keep = jax.random.split(key, 3)
    blocks = EDGES // 128
    per_device = EDGE_DEV // 128
    counts = jax.random.randint(key_count, (blocks,), 1, 129)
    levels = jax.random.randint(key_level, (N_SPACE * N_GRP,), 0, 3)
    keeps = jax.random.randint(key_keep, (blocks,), 0, 4)
    owner = jnp.arange(blocks) // per_device
    kept = keeps >= levels[owner]
    position = jnp.arange(128)
    live = (position[None, :] < counts[:, None]) & kept[:, None]
    return live.astype(jnp.int32).reshape(EDGES)


def draw_send_rows(key, part):
    key = jax.random.fold_in(key, 13)
    devices = N_SPACE * N_GRP
    perms = jax.vmap(lambda k: jax.random.permutation(k, ATOM_DEV))(jax.random.split(key, devices))
    return perms[:, :SLOTS].astype(jnp.int32)


def place_ends(values, own_key, low, largest):
    longest = values.shape.index(max(values.shape))
    spots = []
    for shift in (0, 1):
        where = [jax.random.randint(jax.random.fold_in(own_key, axis), (), 0, length) for axis, length in enumerate(values.shape)]
        where[longest] = (where[longest] + shift) % values.shape[longest]
        spots.append(tuple(where))
    return values.at[spots[0]].set(low).at[spots[1]].set(largest)


def block_scale(key, shape, shards, least, top_value):
    loudness, own = 1.0, jax.random.fold_in(key, 6)
    for dim, shards_of in shards:
        draws = jnp.exp(jax.random.uniform(jax.random.fold_in(own, dim), (shards_of,), jnp.float32, least / len(shards), top_value / len(shards)))
        loudness = loudness * jnp.repeat(draws, shape[dim] // shards_of).reshape([-1 if axis == dim else 1 for axis in range(len(shape))])
    return loudness


def gaussian(key, dims, width, reach, pieces=(), kind=jnp.bfloat16):
    values = width * jax.random.normal(key, dims, jnp.float32)
    if pieces:
        values = values * block_scale(key, dims, pieces, -0.22, 0.18)
    return jnp.clip(values, -reach, reach).astype(kind)


def setup_inputs(seed: int = 0) -> dict:
    splits = jax.random.split(jax.random.key(seed), 16)
    rel_vec = draw_rel_vec(jax.random.fold_in(splits[15], 71), 0)
    atom_feat = gaussian(splits[1], (ATOMS, D), 1.0, 6.0, ((0, 128),))
    centre = place_ends(jax.random.randint(splits[2], (EDGES,), 0, ATOM_DEV), jax.random.fold_in(splits[2], 1), 0, ATOM_DEV - 1).astype(jnp.int32)
    nbr_slot = draw_nbr_slot(jax.random.fold_in(splits[15], 71), 0)
    edge_mask = draw_edge_mask(jax.random.fold_in(splits[15], 71), 0)
    send_rows = draw_send_rows(jax.random.fold_in(splits[15], 71), 0)
    w_radial = gaussian(splits[6], (NB, D), NB ** -0.5, 2.0, (), jnp.float32)
    w_centre = gaussian(splits[7], (D, D), D ** -0.5, 0.375)
    w_nbr = gaussian(splits[8], (D, D), D ** -0.5, 0.375)
    w_env = gaussian(splits[9], (D, C), D ** -0.5, 0.375)
    w_val = gaussian(splits[10], (D, C), D ** -0.5, 0.375)
    w_mix = gaussian(splits[11], (D, D), D ** -0.5, 0.375)
    w_scal = gaussian(splits[12], (3 * C, D), (3 * C) ** -0.5, 0.4375)
    w_read = gaussian(splits[13], (D, D), D ** -0.5, 0.375)
    w_out = gaussian(splits[14], (D,), D ** -0.5, 0.375, (), jnp.float32)
    return {"rel_vec": rel_vec, "atom_feat": atom_feat, "centre": centre, "nbr_slot": nbr_slot, "edge_mask": edge_mask, "send_rows": send_rows, "w_radial": w_radial, "w_centre": w_centre, "w_nbr": w_nbr, "w_env": w_env, "w_val": w_val, "w_mix": w_mix, "w_scal": w_scal, "w_read": w_read, "w_out": w_out}


def harmonics(unit):
    xs, ys, zs = (unit[0], unit[1], unit[2])
    root3 = math.sqrt(3.0)
    root15 = math.sqrt(15.0)
    root5 = math.sqrt(5.0)
    return jnp.stack([jnp.ones_like(xs), root3 * xs, root3 * ys, root3 * zs, root15 * xs * ys, root15 * ys * zs, 0.5 * root5 * (3.0 * zs * zs - 1.0), root15 * xs * zs, 0.5 * root15 * (xs * xs - ys * ys)], axis=0)

def edge_energies(vec, pre, centre, maskf, atoms, w_radial, w_env, w_val, w_mix, w_scal, w_read, w_out):
    cutoff = 5.0
    count = vec.shape[1]
    dist = jnp.sqrt(lax.optimization_barrier(jnp.sum(vec * vec, axis=0)))
    harm = harmonics(vec / dist[None, :])
    ratio = dist / cutoff
    envelope = 1.0 - 28.0 * ratio ** 6 + 48.0 * ratio ** 7 - 21.0 * ratio ** 8
    orders = jnp.arange(1, w_radial.shape[0] + 1).astype(jnp.float32)
    radial = math.sqrt(2.0 / cutoff) * jnp.sin(orders[:, None] * math.pi * ratio[None, :]) / dist[None, :]
    lifted = jnp.dot(radial.T, w_radial, precision=lax.Precision.HIGHEST) + pre
    latent = (jax.nn.silu(lifted) * envelope[:, None]).astype(jnp.bfloat16)
    weights = jnp.dot(latent, w_env, preferred_element_type=jnp.float32) * maskf[:, None]
    values = jnp.dot(latent, w_val, preferred_element_type=jnp.float32)
    chan = w_env.shape[1]
    spread = (harm.T[:, :, None] * weights[:, None, :]).reshape(count, 9 * chan)
    env = jax.ops.segment_sum(spread, centre, num_segments=atoms) * 0.125
    local = env[centre].reshape(count, 9, chan) * harm.T[:, :, None]
    scal = jnp.concatenate([local[:, 0] * values, lax.optimization_barrier(jnp.sum(local[:, 1:4], axis=1)) * values, lax.optimization_barrier(jnp.sum(local[:, 4:9], axis=1)) * values], axis=1).astype(jnp.bfloat16)
    update = jnp.dot(latent, w_mix, preferred_element_type=jnp.float32) + jnp.dot(scal, w_scal, preferred_element_type=jnp.float32)
    mixed = (latent.astype(jnp.float32) + jax.nn.silu(update)).astype(jnp.bfloat16)
    hidden = jax.nn.silu(jnp.dot(mixed, w_read, preferred_element_type=jnp.float32))
    energy = lax.optimization_barrier(jnp.sum(hidden * w_out[None, :], axis=1)) * maskf
    return jax.ops.segment_sum(energy, centre, num_segments=atoms)

def reference(rel_vec, atom_feat, centre, nbr_slot, edge_mask, send_rows, w_radial, w_centre, w_nbr, w_env, w_val, w_mix, w_scal, w_read, w_out):
    centre_proj = jnp.dot(atom_feat, w_centre, preferred_element_type=jnp.float32)
    offsets_a = jnp.array([-1, -1, -1, 0, 0, 1, 1, 1], dtype=jnp.int32)
    offsets_b = jnp.array([-1, 0, 1, -1, 1, -1, 0, 1], dtype=jnp.int32)

    def per_device(carry, dev):
        first = (dev * EDGE_DEV).astype(jnp.int32)
        vec = lax.dynamic_slice_in_dim(rel_vec, first, EDGE_DEV, 1)
        cen = lax.dynamic_slice_in_dim(centre, first, EDGE_DEV, 0)
        slot = lax.dynamic_slice_in_dim(nbr_slot, first, EDGE_DEV, 0)
        maskf = lax.dynamic_slice_in_dim(edge_mask, first, EDGE_DEV, 0).astype(jnp.float32)
        space_idx = dev // N_GRP
        grp_idx = dev % N_GRP
        owners = ((space_idx + offsets_a) % N_SPACE * N_GRP + (grp_idx + offsets_b) % N_GRP).astype(jnp.int32)
        remote_rows = (owners[:, None] * ATOM_DEV + send_rows[owners]).reshape(-1).astype(jnp.int32)
        own_rows = (dev * ATOM_DEV + jnp.arange(ATOM_DEV, dtype=jnp.int32)).astype(jnp.int32)
        table_rows = jnp.concatenate([own_rows, remote_rows]).astype(jnp.int32)
        nbr_proj = jnp.dot(atom_feat[table_rows], w_nbr, preferred_element_type=jnp.float32)
        own = lax.dynamic_slice_in_dim(centre_proj, (dev * ATOM_DEV).astype(jnp.int32), ATOM_DEV, 0)
        pre = own[cen] + nbr_proj[slot]

        def energy_of(vectors):
            return edge_energies(vectors, pre, cen, maskf, ATOM_DEV, w_radial, w_env, w_val, w_mix, w_scal, w_read, w_out)
        energies, pull = jax.vjp(energy_of, vec)
        grad = pull(jnp.ones_like(energies))[0]
        centre_force = jax.ops.segment_sum(grad.T, cen, num_segments=ATOM_DEV).T
        away = jax.ops.segment_sum(grad.T, table_rows[slot], num_segments=ATOMS).T
        return (carry + away, (energies, centre_force))
    start = jnp.zeros((3, ATOMS), jnp.float32)
    away, (energies, centre_force) = lax.scan(per_device, start, jnp.arange(N_SPACE * N_GRP, dtype=jnp.int32))
    atom_energy = energies.reshape(ATOMS)
    forces = jnp.transpose(centre_force, (1, 0, 2)).reshape(3, ATOMS) - away
    return (atom_energy, forces)
```

```python
import functools
import math

import jax
import jax.numpy as jnp
from jax import lax
from jax.experimental import pallas as pl
from jax.experimental.pallas import tpu as pltpu
from jax.sharding import PartitionSpec as P

F32 = jnp.float32
BF16 = jnp.bfloat16
MESH = pl.DeviceIdType.MESH
OFFSETS = ((-1, -1), (-1, 0), (-1, 1), (0, -1), (0, 1), (1, -1), (1, 0), (1, 1))
CUTOFF = 5.0
R3, R5, R15 = math.sqrt(3.0), math.sqrt(5.0), math.sqrt(15.0)
DEGREES = ((0,), (1, 2, 3), (4, 5, 6, 7, 8))
WIDTH = 256
C = 64


def mm(lhs, rhs):
    return jnp.dot(lhs, rhs, preferred_element_type=F32)


def mm_nt(lhs, rhs):
    return lax.dot_general(lhs, rhs, (((1,), (1,)), ((), ())), preferred_element_type=F32)


def turned(block):
    return block.astype(F32).T.astype(BF16)


def neighbours(space, grp):
    me_s, me_g = lax.axis_index("space"), lax.axis_index("grp")
    return [(lax.rem(me_s + a + space, space), lax.rem(me_g + b + grp, grp)) for a, b in OFFSETS]


def onehot(row, count, first=0):
    ids = lax.broadcasted_iota(jnp.int32, (count, row.shape[1]), 0) + first
    return jnp.where(ids == row, 1.0, 0.0).astype(BF16)


def greet(peers):
    barrier = pltpu.get_barrier_semaphore()
    for peer in peers:
        pl.semaphore_signal(barrier, inc=1, device_id=peer, device_id_type=MESH)
    return barrier


def exchange(peers, source, landing, send_sem, recv_sem):
    return [
        pltpu.make_async_remote_copy(
            src_ref=source(c),
            dst_ref=landing.at[7 - c],
            send_sem=send_sem.at[c],
            recv_sem=recv_sem.at[7 - c],
            device_id=peer,
            device_id_type=MESH,
        )
        for c, peer in enumerate(peers)
    ]


def geometry(vec_ref, centre_ref, slot_ref, geo_ref, dense):
    for i in range(3):
        for b in range(16):
            dense[i, b : b + 1, :] = vec_ref[i : i + 1, b * 128 : (b + 1) * 128]
    vx, vy, vz = dense[0], dense[1], dense[2]
    dist = jnp.sqrt(vx * vx + vy * vy + vz * vz)
    inv = 1.0 / dist
    t = dist / CUTOFF
    angle = math.pi * t
    sin1, cos1 = jnp.sin(angle), jnp.cos(angle)
    scale = math.sqrt(2.0 / CUTOFF)
    sins, coss = [jnp.zeros_like(t), sin1], [jnp.ones_like(t), cos1]
    for n in range(2, 9):
        sins.append(2.0 * cos1 * sins[-1] - sins[-2])
        coss.append(2.0 * cos1 * coss[-1] - coss[-2])
    for n in range(1, 9):
        radial = scale * sins[n] * inv
        geo_ref[0, :, n - 1, :] = radial
        geo_ref[1, :, n - 1, :] = (scale * n * math.pi / CUTOFF * coss[n] - radial) * inv
    t2 = t * t
    t4 = t2 * t2
    t5, t6, t7, t8 = t4 * t, t4 * t2, t4 * t2 * t, t4 * t4
    geo_ref[2, :, 0, :] = vx * inv
    geo_ref[2, :, 1, :] = vy * inv
    geo_ref[2, :, 2, :] = vz * inv
    geo_ref[2, :, 3, :] = inv
    geo_ref[2, :, 4, :] = 1.0 - 28.0 * t6 + 48.0 * t7 - 21.0 * t8
    geo_ref[2, :, 5, :] = (336.0 * t6 - 168.0 * t5 - 168.0 * t7) / CUTOFF
    geo_ref[2, :, 6, :] = centre_ref[...].astype(F32)
    geo_ref[2, :, 7, :] = slot_ref[...].astype(F32)


def first_kernel(
    space, grp,
    vec_ref, feat_ref, centre_ref, slot_ref, rows_ref, w_radial_ref, w_centre_ref, w_nbr_ref, w_env_ref, w_val_ref,
    w_mix_ref, w_scal_ref, w_read_ref, w_out_ref,
    tab_ref, own_ref, cen_ref, geo_ref, wr_ref, wrhl_ref, wev_ref, wevt_ref, wmixt_ref, wscalt_ref, wreadt_ref, wout_ref,
    outgoing, dense, send_sem, recv_sem,
):
    peers = neighbours(space, grp)
    barrier = greet(peers)
    own = mm(feat_ref[...], w_nbr_ref[...]).T.astype(BF16)
    own_ref[...] = own
    outgoing[...] = mm(own, onehot(rows_ref[...], WIDTH)).astype(BF16)
    pl.semaphore_wait(barrier, 8)
    copies = exchange(peers, lambda c: outgoing, tab_ref, send_sem, recv_sem)
    for copy in copies:
        copy.start()
    cen_ref[...] = mm(feat_ref[...], w_centre_ref[...]).T.astype(BF16)
    geometry(vec_ref, centre_ref, slot_ref, geo_ref, dense)
    w_radial = w_radial_ref[...]
    high = w_radial.astype(BF16).astype(F32)
    low = w_radial - high
    stacked = jnp.concatenate([high, low, high, jnp.zeros((104, WIDTH), F32)], axis=0)
    wr_ref[...] = stacked.T[:, :32].astype(BF16)
    wrhl_ref[...] = jnp.concatenate([high, low], axis=0).astype(BF16)
    both = jnp.concatenate([w_env_ref[...].astype(F32), w_val_ref[...].astype(F32)], axis=1)
    wev_ref[...] = both.astype(BF16)
    wevt_ref[...] = both.T.astype(BF16)
    wmixt_ref[...] = turned(w_mix_ref[...])
    scal = jnp.concatenate([w_scal_ref[...].astype(F32), jnp.zeros((64, WIDTH), F32)], axis=0)
    wscalt_ref[...] = scal.T[:, :192].astype(BF16)
    wreadt_ref[...] = turned(w_read_ref[...])
    wout_ref[...] = jnp.broadcast_to(w_out_ref[...], (128, WIDTH)).T
    for copy in copies:
        copy.wait_send()
        copy.wait_recv()


def harmonics(x, y, z):
    return [
        None, R3 * x, R3 * y, R3 * z,
        R15 * x * y, R15 * y * z, 0.5 * R5 * (3.0 * z * z - 1.0), R15 * x * z, 0.5 * R15 * (x * x - y * y),
    ]


def scaled(block, harm):
    return block if harm is None else block * harm


def part(block, i):
    return block[i * C : (i + 1) * C]


def down(block):
    return jnp.sum(block, axis=0, keepdims=True)


def compact(mask_ref, geo_ref, packed):
    packed[0] = jnp.zeros_like(packed[0])
    packed[1] = jnp.zeros_like(packed[1])
    sub = lax.broadcasted_iota(jnp.int32, packed.shape[1:], 1)
    packed[2] = jnp.where(sub >= 6, -1.0, 0.0)
    lane = lax.broadcasted_iota(jnp.int32, (8, 128), 1)
    start = jnp.int32(0)
    for b in range(16):
        count = jnp.sum(mask_ref[b : b + 1, :].astype(F32)).astype(jnp.int32)
        row, shift = lax.shift_right_logical(start, 7), lax.bitwise_and(start, 127)
        here = (lane >= shift) & (lane < shift + count)
        spill = lane < shift + count - 128
        for g in range(3):
            moved = pltpu.roll(geo_ref[g, b], shift, 1)
            packed[g, row] = jnp.where(here, moved, packed[g, row])
            packed[g, row + 1] = jnp.where(spill, moved, packed[g, row + 1])
        start = start + count
    return start


def main_kernel(
    span,
    mask_ref, geo_ref, tab_ref, own_ref, cen_ref, wr_ref, wrhl_ref, wev_ref, wevt_ref, wmixt_ref, wscalt_ref, wreadt_ref,
    wout_ref, w_mix_ref, w_scal_ref, w_read_ref,
    energy_ref, force_ref, sums_ref,
    packed, lat_s, act_s, slope_s, wv_s, back_s, vbar_s, hbar_s, en_s, env_s, envbar_s, envh_s, fsum, csum,
):
    wide = span // 128
    total = compact(mask_ref, geo_ref, packed)
    chunks = lax.div(total + (span - 1), span)
    env_s[...] = jnp.zeros_like(env_s)
    envbar_s[...] = jnp.zeros_like(envbar_s)
    fsum[...] = jnp.zeros_like(fsum)
    csum[...] = jnp.zeros_like(csum)

    def rows(group, j):
        return jnp.concatenate([packed[group, wide * j + i] for i in range(wide)], axis=1)

    def fields(j):
        geo = rows(2, j)
        return [geo[i : i + 1] for i in range(8)]

    def forward(j, carry):
        x, y, z, _, envelope, _, centre, slot = fields(j)
        centre, slot = centre.astype(jnp.int32), slot.astype(jnp.int32)
        radial = rows(0, j)
        high = radial.astype(BF16).astype(F32)
        stacked = jnp.concatenate([high, high, radial - high, jnp.zeros_like(high)], axis=0).astype(BF16)
        hot = onehot(centre, WIDTH)
        lifted = mm(wr_ref[...], stacked) + mm(cen_ref[...], hot) + mm(own_ref[...], onehot(slot, WIDTH))
        for pair in range(4):
            block = jnp.concatenate([tab_ref[2 * pair], tab_ref[2 * pair + 1]], axis=1)
            lifted = lifted + mm(block, onehot(slot, WIDTH, WIDTH * (pair + 1)))
        gate = 1.0 / (1.0 + jnp.exp(-lifted))
        active = lifted * gate
        act_s[j] = active
        slope_s[j] = gate + active * (1.0 - gate)
        latent = (active * envelope).astype(BF16)
        lat_s[j] = latent
        wv = mm(wevt_ref[...], latent)
        wv_s[j] = wv
        weights = wv[:C]
        harm = harmonics(x, y, z)
        spread = jnp.concatenate([scaled(weights, harm[i]).astype(BF16) for i in range(9)], axis=0)
        env_s[...] += mm_nt(spread, hot)
        return carry

    lax.fori_loop(0, chunks, forward, 0)
    envh_s[...] = (env_s[...] * 0.125).astype(BF16)

    def middle(j, carry):
        x, y, z, _, _, _, centre, _ = fields(j)
        hot = onehot(centre.astype(jnp.int32), WIDTH)
        harm = harmonics(x, y, z)
        local = mm(envh_s[...], hot)
        values = wv_s[j, C:]
        invariants = []
        for degree in DEGREES:
            whole = None
            for i in degree:
                term = scaled(part(local, i), harm[i])
                whole = term if whole is None else whole + term
            invariants.append(whole)
        scal = jnp.concatenate([(q * values).astype(BF16) for q in invariants], axis=0)
        latent = lat_s[j]
        update = mm(wmixt_ref[...], latent) + mm(wscalt_ref[...], scal)
        gate = 1.0 / (1.0 + jnp.exp(-update))
        active = update * gate
        slope = gate + active * (1.0 - gate)
        mixed = (latent.astype(F32) + active).astype(BF16)
        hidden = mm(wreadt_ref[...], mixed)
        gate_h = 1.0 / (1.0 + jnp.exp(-hidden))
        active_h = hidden * gate_h
        out = jnp.concatenate([wout_ref[...]] * wide, axis=1)
        en_s[j] = down(active_h * out)
        hidden_bar = (out * (gate_h + active_h * (1.0 - gate_h))).astype(BF16)
        mixed_bar = mm(w_read_ref[...], hidden_bar).astype(BF16).astype(F32)
        update_bar = (mixed_bar * slope).astype(BF16)
        back_s[j] = mixed_bar + mm(w_mix_ref[...], update_bar)
        scal_bar = mm(w_scal_ref[...], update_bar)
        values_bar = None
        locals_bar, harm_bar = [], []
        for level, degree in enumerate(DEGREES):
            bar = part(scal_bar, level)
            term = bar * invariants[level]
            values_bar = term if values_bar is None else values_bar + term
            inner = bar * values
            for i in degree:
                locals_bar.append(scaled(inner, harm[i]).astype(BF16))
                if i:
                    harm_bar.append(down(part(local, i) * inner))
        vbar_s[j] = values_bar.astype(BF16)
        hbar_s[j] = jnp.concatenate(harm_bar, axis=0)
        envbar_s[...] += mm_nt(jnp.concatenate(locals_bar, axis=0), hot)
        return carry

    lax.fori_loop(0, chunks, middle, 0)
    envh_s[...] = (envbar_s[...] * 0.125).astype(BF16)

    def backward(j, carry):
        x, y, z, inv, envelope, slope_env, centre, slot = fields(j)
        slot = slot.astype(jnp.int32)
        hot = onehot(centre.astype(jnp.int32), WIDTH)
        harm = harmonics(x, y, z)
        spread_bar = mm(envh_s[...], hot)
        weights = wv_s[j, :C]
        weights_bar = part(spread_bar, 0)
        for i in range(1, 9):
            weights_bar = weights_bar + part(spread_bar, i) * harm[i]
        harm_bar = hbar_s[j]
        bars = [None] + [harm_bar[i - 1 : i] + down(part(spread_bar, i) * weights) for i in range(1, 9)]
        wv_bar = jnp.concatenate([weights_bar.astype(BF16), vbar_s[j]], axis=0)
        latent_bar = back_s[j] + mm(wev_ref[...], wv_bar)
        envelope_bar = down(latent_bar * act_s[j])
        lifted_bar = (latent_bar * envelope * slope_s[j]).astype(BF16)
        radial_bar = mm(wrhl_ref[...], lifted_bar)
        dist_bar = down((radial_bar[:8] + radial_bar[8:]) * rows(1, j)) + envelope_bar * slope_env
        ux = R3 * bars[1] + R15 * (y * bars[4] + z * bars[7] + x * bars[8])
        uy = R3 * bars[2] + R15 * (x * bars[4] + z * bars[5] - y * bars[8])
        uz = R3 * bars[3] + R15 * (y * bars[5] + x * bars[7]) + 3.0 * R5 * z * bars[6]
        along = dist_bar - (x * ux + y * uy + z * uz) * inv
        grads = jnp.concatenate([ux * inv + x * along, uy * inv + y * along, uz * inv + z * along, en_s[j]], axis=0)
        top = grads.astype(BF16).astype(F32)
        both = jnp.concatenate([top, grads - top], axis=0)
        csum[...] += mm_nt(both.astype(BF16), hot)
        block = lax.shift_right_arithmetic(slot, 7)
        lo = onehot(lax.bitwise_and(slot, 127), 128)
        split = jnp.concatenate([jnp.where(block == h, both, 0.0) for h in range(10)], axis=0).astype(BF16)
        fsum[...] += mm_nt(split, lo)
        return carry

    lax.fori_loop(0, chunks, backward, 0)
    centre_sum = csum[0:4] + csum[4:8]
    energy_ref[...] = centre_sum[3:4]
    own = jnp.concatenate([fsum[0:4] + fsum[4:8], fsum[8:12] + fsum[12:16]], axis=1)
    force_ref[...] = (centre_sum - own)[0:3]
    for c in range(8):
        first = 16 + 8 * c
        sums_ref[c, 0:4] = fsum[first : first + 4] + fsum[first + 4 : first + 8]
        sums_ref[c, 4:8] = jnp.zeros((4, 128), F32)


def last_kernel(space, grp, sums_ref, force_ref, rows_ref, out_ref, landed, send_sem, recv_sem):
    peers = neighbours(space, grp)
    barrier = greet(peers)
    pl.semaphore_wait(barrier, 8)
    copies = exchange(peers, lambda c: sums_ref.at[c], landed, send_sem, recv_sem)
    for copy in copies:
        copy.start()
    hot = onehot(rows_ref[...], WIDTH)
    for copy in copies:
        copy.wait_send()
        copy.wait_recv()
    total = landed[0]
    for c in range(1, 8):
        total = total + landed[c]
    top = total.astype(BF16).astype(F32)
    both = jnp.concatenate([top, total - top], axis=0).astype(BF16)
    away = mm_nt(both, hot)
    out_ref[...] = force_ref[...] - (away[0:3] + away[8:11])


def per_device(
    space, grp,
    rel_vec, atom_feat, centre, nbr_slot, edge_mask, send_rows, w_radial, w_centre, w_nbr, w_env, w_val, w_mix, w_scal,
    w_read, w_out,
):
    span = 256
    chunks = 2048 // span
    vmem = pl.BlockSpec(memory_space=pltpu.VMEM)
    shape = jax.ShapeDtypeStruct
    limit = 56 * 1024 * 1024
    tab, own, cen, geo, wr, wrhl, wev, wevt, wmixt, wscalt, wreadt, wout = pl.pallas_call(
        functools.partial(first_kernel, space, grp),
        out_shape=[
            shape((8, WIDTH, 128), BF16), shape((WIDTH, WIDTH), BF16), shape((WIDTH, WIDTH), BF16), shape((3, 16, 8, 128), F32),
            shape((WIDTH, 32), BF16), shape((16, WIDTH), BF16), shape((WIDTH, 128), BF16), shape((128, WIDTH), BF16),
            shape((WIDTH, WIDTH), BF16), shape((WIDTH, 192), BF16), shape((WIDTH, WIDTH), BF16), shape((WIDTH, 128), F32),
        ],
        in_specs=[vmem] * 14,
        out_specs=[vmem] * 12,
        scratch_shapes=[
            pltpu.VMEM((WIDTH, 128), BF16),
            pltpu.VMEM((3, 16, 128), F32),
            pltpu.SemaphoreType.DMA((8,)),
            pltpu.SemaphoreType.DMA((8,)),
        ],
        compiler_params=pltpu.CompilerParams(collective_id=0, has_side_effects=True, vmem_limit_bytes=limit),
        name="exchange_rows",
    )(
        rel_vec, atom_feat, centre.reshape(16, 128), nbr_slot.reshape(16, 128), send_rows, w_radial, w_centre, w_nbr, w_env,
        w_val, w_mix, w_scal, w_read, w_out.reshape(1, WIDTH),
    )
    energy, force, sums = pl.pallas_call(
        functools.partial(main_kernel, span),
        out_shape=[shape((1, WIDTH), F32), shape((3, WIDTH), F32), shape((8, 8, 128), F32)],
        in_specs=[vmem] * 16,
        out_specs=[vmem] * 3,
        scratch_shapes=[
            pltpu.VMEM((3, 18, 8, 128), F32),
            pltpu.VMEM((chunks, WIDTH, span), BF16),
            pltpu.VMEM((chunks, WIDTH, span), F32),
            pltpu.VMEM((chunks, WIDTH, span), F32),
            pltpu.VMEM((chunks, 2 * C, span), F32),
            pltpu.VMEM((chunks, WIDTH, span), F32),
            pltpu.VMEM((chunks, C, span), BF16),
            pltpu.VMEM((chunks, 8, span), F32),
            pltpu.VMEM((chunks, 1, span), F32),
            pltpu.VMEM((9 * C, WIDTH), F32),
            pltpu.VMEM((9 * C, WIDTH), F32),
            pltpu.VMEM((9 * C, WIDTH), BF16),
            pltpu.VMEM((80, 128), F32),
            pltpu.VMEM((8, WIDTH), F32),
        ],
        compiler_params=pltpu.CompilerParams(vmem_limit_bytes=limit),
        name="edges",
    )(edge_mask.reshape(16, 128), geo, tab, own, cen, wr, wrhl, wev, wevt, wmixt, wscalt, wreadt, wout, w_mix, w_scal, w_read)
    forces = pl.pallas_call(
        functools.partial(last_kernel, space, grp),
        out_shape=shape((3, WIDTH), F32),
        in_specs=[vmem] * 3,
        out_specs=vmem,
        scratch_shapes=[
            pltpu.VMEM((8, 8, 128), F32),
            pltpu.SemaphoreType.DMA((8,)),
            pltpu.SemaphoreType.DMA((8,)),
        ],
        compiler_params=pltpu.CompilerParams(collective_id=1, has_side_effects=True, vmem_limit_bytes=limit),
        name="return_sums",
    )(sums, force, send_rows)
    return (energy.reshape(WIDTH), forces)


def solution(mesh):
    edges = P(("space", "grp"))
    placed = (
        P(None, ("space", "grp")), P(("space", "grp"), None), edges, edges, edges, P(("space", "grp"), None),
    ) + (P(),) * 9
    return jax.shard_map(
        functools.partial(per_device, mesh.shape["space"], mesh.shape["grp"]),
        mesh=mesh,
        in_specs=placed,
        out_specs=(edges, P(None, ("space", "grp"))),
        check_vma=False,
    )
```

```python
import functools
import math

import jax
import jax.numpy as jnp
from jax import lax
from jax.experimental import pallas as pl
from jax.experimental.pallas import tpu as pltpu
from jax.sharding import PartitionSpec as P

F32 = jnp.float32
BF16 = jnp.bfloat16
MESH = pl.DeviceIdType.MESH
OFFSETS = ((-1, -1), (-1, 0), (-1, 1), (0, -1), (0, 1), (1, -1), (1, 0), (1, 1))
STAGES = ((3, 4), (1, 6), (0, 2, 5, 7))
CUTOFF = 5.0
R3, R5, R15 = math.sqrt(3.0), math.sqrt(5.0), math.sqrt(15.0)
DEGREES = ((0,), (1, 2, 3), (4, 5, 6, 7, 8))
WIDTH = 256
EDGES = 2048
C = 64


def mm(lhs, rhs):
    return jnp.dot(lhs, rhs, preferred_element_type=F32)


def mm_nt(lhs, rhs):
    return lax.dot_general(lhs, rhs, (((1,), (1,)), ((), ())), preferred_element_type=F32)


def turned(block):
    return block.astype(F32).T.astype(BF16)


def sigmoid(x):
    return 0.5 + 0.5 * jnp.tanh(0.5 * x)


def onehot(row, count, first=0):
    ids = lax.broadcasted_iota(jnp.int16, (count, row.shape[1]), 0)
    own = (row - first).astype(jnp.int16)
    return jnp.where(ids == own, jnp.bfloat16(1.0), jnp.bfloat16(0.0))


def down(block):
    return jnp.sum(block, axis=0, keepdims=True)


def part(block, i):
    return block[i * C : (i + 1) * C]


def scaled(block, harm):
    return block if harm is None else block * harm


def harmonics(x, y, z):
    return [
        None, R3 * x, R3 * y, R3 * z,
        R15 * x * y, R15 * y * z, 0.5 * R5 * (3.0 * z * z - 1.0), R15 * x * z, 0.5 * R15 * (x * x - y * y),
    ]


def geometry(vec, centre, slot, mask, geo, dense):
    for i in range(3):
        for b in range(16):
            dense[i, b : b + 1, :] = vec[i : i + 1, b * 128 : (b + 1) * 128]
    real = mask[...] > 0
    vx, vy, vz = [jnp.where(real, dense[i], 1.0) for i in range(3)]
    dist = jnp.sqrt(vx * vx + vy * vy + vz * vz)
    inv = 1.0 / dist
    t = dist / CUTOFF
    angle = math.pi * t
    sin1, cos1 = jnp.sin(angle), jnp.cos(angle)
    scale = math.sqrt(2.0 / CUTOFF)
    sins, coss = [jnp.zeros_like(t), sin1], [jnp.ones_like(t), cos1]
    for n in range(2, 9):
        sins.append(2.0 * cos1 * sins[-1] - sins[-2])
        coss.append(2.0 * cos1 * coss[-1] - coss[-2])
    for n in range(1, 9):
        radial = scale * sins[n] * inv
        geo[0, :, n - 1, :] = radial
        geo[1, :, n - 1, :] = (scale * n * math.pi / CUTOFF * coss[n] - radial) * inv
    t2 = t * t
    t4 = t2 * t2
    t5, t6, t7, t8 = t4 * t, t4 * t2, t4 * t2 * t, t4 * t4
    geo[2, :, 0, :] = vx * inv
    geo[2, :, 1, :] = vy * inv
    geo[2, :, 2, :] = vz * inv
    geo[2, :, 3, :] = inv
    geo[2, :, 4, :] = 1.0 - 28.0 * t6 + 48.0 * t7 - 21.0 * t8
    geo[2, :, 5, :] = (336.0 * t6 - 168.0 * t5 - 168.0 * t7) / CUTOFF
    geo[2, :, 6, :] = jnp.where(real, centre[...], -1).astype(F32)
    geo[2, :, 7, :] = jnp.where(real, slot[...], -1).astype(F32)


def kernel(
    space, grp, span,
    vec_in, feat_in, centre_in, slot_in, mask_in, rows_in, w_radial_in, w_centre_in, w_nbr_in, w_env_in, w_val_in,
    w_mix_in, w_scal_in, w_read_in, w_out_in,
    energy_ref, force_ref,
    vec, feat, centre, slot, mask, send_rows, w_radial, w_centre, w_nbr, wevt, w_mix, w_scal, w_read, w_out,
    outgoing, tab, near, geo, dense, wr, wrhl, wev, wmixt, wscalt, wreadt, wout,
    lat_s, act_s, slope_s, wv_s, back_s, vbar_s, hbar_s, en_s, env_s, envh_s, fsum, csum, leaving, landed,
    in_sem, send_sem, recv_sem, send_sem2, recv_sem2,
):
    wide = span // 128
    chunks = EDGES // span
    me_s, me_g = lax.axis_index("space"), lax.axis_index("grp")
    peers = [(lax.rem(me_s + a + space, space), lax.rem(me_g + b + grp, grp)) for a, b in OFFSETS]
    barrier = pltpu.get_barrier_semaphore()
    for peer in peers:
        pl.semaphore_signal(barrier, inc=1, device_id=peer, device_id_type=MESH)
    pairs = [
        (feat_in, feat), (w_nbr_in, w_nbr), (rows_in, send_rows), (w_centre_in, w_centre), (vec_in, vec), (centre_in, centre),
        (slot_in, slot), (mask_in, mask), (w_radial_in, w_radial), (w_env_in, wevt.at[0:C]), (w_val_in, wevt.at[C : 2 * C]),
        (w_mix_in, w_mix), (w_scal_in, w_scal), (w_read_in, w_read), (w_out_in, w_out),
    ]
    loads = [pltpu.make_async_copy(a, b, in_sem.at[i]) for i, (a, b) in enumerate(pairs)]
    for load in loads:
        load.start()
    for load in loads[:3]:
        load.wait()
    own = mm(feat[...], w_nbr[...]).T.astype(BF16)
    near[:, 0:WIDTH] = own
    outgoing[...] = mm(own, onehot(send_rows[...], WIDTH)).astype(BF16)
    pl.semaphore_wait(barrier, 8)

    def remote(c, source, landing, sends, receives):
        return pltpu.make_async_remote_copy(
            src_ref=source,
            dst_ref=landing.at[7 - c],
            send_sem=sends.at[c],
            recv_sem=receives.at[7 - c],
            device_id=peers[c],
            device_id_type=MESH,
        )

    copies = [remote(c, outgoing, tab, send_sem, recv_sem) for c in range(8)]
    for stage in STAGES:
        for c in stage:
            copies[c].start()
    for load in loads[3:]:
        load.wait()
    near[:, WIDTH:] = mm(feat[...], w_centre[...]).T.astype(BF16)
    geometry(vec, centre, slot, mask, geo, dense)
    high = w_radial[...].astype(BF16).astype(F32)
    low = w_radial[...] - high
    stacked = jnp.concatenate([high, low, high, jnp.zeros((104, WIDTH), F32)], axis=0)
    wr[...] = stacked.T[:, :32].astype(BF16)
    wrhl[...] = jnp.concatenate([high, low], axis=0).astype(BF16)

    def rows(group, j):
        return jnp.concatenate([geo[group, wide * j + i] for i in range(wide)], axis=1)

    def fields(j):
        block = rows(2, j)
        return [block[i : i + 1] for i in range(8)]

    def index(row):
        return row.astype(jnp.int32)

    for j in range(chunks):
        radial = rows(0, j)
        top = radial.astype(BF16).astype(F32)
        terms = jnp.concatenate([top, top, radial - top, jnp.zeros_like(top)], axis=0).astype(BF16)
        marks = fields(j)
        hot = jnp.concatenate([onehot(index(marks[7]), WIDTH), onehot(index(marks[6]), WIDTH)], axis=0)
        act_s[j] = mm(near[...], hot) + mm(wr[...], terms)

    wev[...] = turned(wevt[...])
    wmixt[...] = turned(w_mix[...])
    padded = jnp.concatenate([w_scal[...].astype(F32), jnp.zeros((C, WIDTH), F32)], axis=0)
    wscalt[...] = padded.T[:, : 3 * C].astype(BF16)
    wreadt[...] = turned(w_read[...])
    wout[...] = jnp.broadcast_to(w_out[...], (128, WIDTH)).T

    def gathered(j, stage):
        slots = index(fields(j)[7])
        hot = jnp.concatenate([onehot(slots, 128, WIDTH + 128 * c) for c in stage], axis=0)
        return act_s[j] + mm(jnp.concatenate([tab[c] for c in stage], axis=1), hot)

    for stage in STAGES[:2]:
        for c in stage:
            copies[7 - c].wait_recv()
        for j in range(chunks):
            act_s[j] = gathered(j, stage)
    for c in STAGES[2]:
        copies[7 - c].wait_recv()

    for j in range(chunks):
        x, y, z, _, envelope, _, centres, _ = fields(j)
        lifted = gathered(j, STAGES[2])
        gate = sigmoid(lifted)
        active = lifted * gate
        act_s[j] = active
        slope_s[j] = gate + active * (1.0 - gate)
        latent = (active * envelope).astype(BF16)
        lat_s[j] = latent
        wv = mm(wevt[...], latent)
        wv_s[j] = wv
        weights = wv[:C]
        harm = harmonics(x, y, z)
        spread = jnp.concatenate([scaled(weights, harm[i]).astype(BF16) for i in range(9)], axis=0)
        term = mm_nt(spread, onehot(index(centres), WIDTH))
        env_s[...] = term if j == 0 else env_s[...] + term
    envh_s[...] = (env_s[...] * 0.125).astype(BF16)

    for j in range(chunks):
        x, y, z, _, _, _, centres, _ = fields(j)
        hot = onehot(index(centres), WIDTH)
        harm = harmonics(x, y, z)
        local = mm(envh_s[...], hot)
        values = wv_s[j, C:]
        invariants = []
        for degree in DEGREES:
            whole = None
            for i in degree:
                term = scaled(part(local, i), harm[i])
                whole = term if whole is None else whole + term
            invariants.append(whole)
        scal = jnp.concatenate([(q * values).astype(BF16) for q in invariants], axis=0)
        latent = lat_s[j]
        update = mm(wmixt[...], latent) + mm(wscalt[...], scal)
        gate = sigmoid(update)
        active = update * gate
        slope = gate + active * (1.0 - gate)
        mixed = (latent.astype(F32) + active).astype(BF16)
        hidden = mm(wreadt[...], mixed)
        gate_h = sigmoid(hidden)
        active_h = hidden * gate_h
        out = jnp.concatenate([wout[...]] * wide, axis=1)
        en_s[j] = down(active_h * out)
        hidden_bar = (out * (gate_h + active_h * (1.0 - gate_h))).astype(BF16)
        mixed_bar = mm(w_read[...], hidden_bar).astype(BF16).astype(F32)
        update_bar = (mixed_bar * slope).astype(BF16)
        back_s[j] = mixed_bar + mm(w_mix[...], update_bar)
        scal_bar = mm(w_scal[...], update_bar)
        values_bar = None
        locals_bar, harm_bar = [], []
        for level, degree in enumerate(DEGREES):
            bar = part(scal_bar, level)
            term = bar * invariants[level]
            values_bar = term if values_bar is None else values_bar + term
            inner = bar * values
            for i in degree:
                locals_bar.append(scaled(inner, harm[i]).astype(BF16))
                if i:
                    harm_bar.append(down(part(local, i) * inner))
        vbar_s[j] = values_bar.astype(BF16)
        hbar_s[j] = jnp.concatenate(harm_bar, axis=0)
        term = mm_nt(jnp.concatenate(locals_bar, axis=0), hot)
        env_s[...] = term if j == 0 else env_s[...] + term
    envh_s[...] = (env_s[...] * 0.125).astype(BF16)

    for j in range(chunks):
        x, y, z, inv, envelope, slope_env, centres, slots = fields(j)
        slots = index(slots)
        hot = onehot(index(centres), WIDTH)
        harm = harmonics(x, y, z)
        spread_bar = mm(envh_s[...], hot)
        weights = wv_s[j, :C]
        weights_bar = part(spread_bar, 0)
        for i in range(1, 9):
            weights_bar = weights_bar + part(spread_bar, i) * harm[i]
        harm_bar = hbar_s[j]
        bars = [None] + [harm_bar[i - 1 : i] + down(part(spread_bar, i) * weights) for i in range(1, 9)]
        wv_bar = jnp.concatenate([weights_bar.astype(BF16), vbar_s[j]], axis=0)
        latent_bar = back_s[j] + mm(wev[...], wv_bar)
        envelope_bar = down(latent_bar * act_s[j])
        lifted_bar = (latent_bar * envelope * slope_s[j]).astype(BF16)
        radial_bar = mm(wrhl[...], lifted_bar)
        dist_bar = down((radial_bar[:8] + radial_bar[8:]) * rows(1, j)) + envelope_bar * slope_env
        ux = R3 * bars[1] + R15 * (y * bars[4] + z * bars[7] + x * bars[8])
        uy = R3 * bars[2] + R15 * (x * bars[4] + z * bars[5] - y * bars[8])
        uz = R3 * bars[3] + R15 * (y * bars[5] + x * bars[7]) + 3.0 * R5 * z * bars[6]
        along = dist_bar - (x * ux + y * uy + z * uz) * inv
        grads = jnp.concatenate([ux * inv + x * along, uy * inv + y * along, uz * inv + z * along, en_s[j]], axis=0)
        top = grads.astype(BF16).astype(F32)
        both = jnp.concatenate([top, grads - top], axis=0)
        block = lax.shift_right_arithmetic(slots, 7)
        low_hot = onehot(lax.bitwise_and(slots, 127), 128)
        split = jnp.concatenate([jnp.where(block == h, both, 0.0) for h in range(10)], axis=0).astype(BF16)
        term, own_term = mm_nt(split, low_hot), mm_nt(both.astype(BF16), hot)
        fsum[...] = term if j == 0 else fsum[...] + term
        csum[...] = own_term if j == 0 else csum[...] + own_term

    for c in range(8):
        first = 16 + 8 * c
        leaving[c, 0:4] = fsum[first : first + 4] + fsum[first + 4 : first + 8]
        leaving[c, 4:8] = jnp.zeros((4, 128), F32)
    returns = [remote(c, leaving.at[c], landed, send_sem2, recv_sem2) for c in range(8)]
    for copy in returns:
        copy.start()
    centre_sum = csum[0:4] + csum[4:8]
    energy_ref[...] = centre_sum[3:4]
    own_sum = jnp.concatenate([fsum[0:4] + fsum[4:8], fsum[8:12] + fsum[12:16]], axis=1)
    hot = onehot(send_rows[...], WIDTH)
    for copy in returns:
        copy.wait_recv()
    total = landed[0]
    for c in range(1, 8):
        total = total + landed[c]
    top = total.astype(BF16).astype(F32)
    away = mm_nt(jnp.concatenate([top, total - top], axis=0).astype(BF16), hot)
    force_ref[...] = (centre_sum - own_sum)[0:3] - (away[0:3] + away[8:11])
    for copy in copies + returns:
        copy.wait_send()


def per_device(
    space, grp,
    rel_vec, atom_feat, centre, nbr_slot, edge_mask, send_rows, w_radial, w_centre, w_nbr, w_env, w_val, w_mix, w_scal,
    w_read, w_out,
):
    span = 1024
    chunks = EDGES // span
    shape = jax.ShapeDtypeStruct
    vm = pltpu.VMEM
    energy, forces = pl.pallas_call(
        functools.partial(kernel, space, grp, span),
        out_shape=[shape((1, WIDTH), F32), shape((3, WIDTH), F32)],
        in_specs=[pl.BlockSpec(memory_space=pl.ANY)] * 15,
        out_specs=[pl.BlockSpec(memory_space=pltpu.VMEM)] * 2,
        scratch_shapes=[
            vm((3, EDGES), F32), vm((WIDTH, WIDTH), BF16), vm((16, 128), jnp.int32), vm((16, 128), jnp.int32),
            vm((16, 128), jnp.int32), vm((1, 128), jnp.int32), vm((8, WIDTH), F32), vm((WIDTH, WIDTH), BF16),
            vm((WIDTH, WIDTH), BF16), vm((2 * C, WIDTH), BF16), vm((WIDTH, WIDTH), BF16), vm((3 * C, WIDTH), BF16),
            vm((WIDTH, WIDTH), BF16), vm((1, WIDTH), F32),
            vm((WIDTH, 128), BF16), vm((8, WIDTH, 128), BF16), vm((WIDTH, 2 * WIDTH), BF16), vm((3, 16, 8, 128), F32),
            vm((3, 16, 128), F32), vm((WIDTH, 32), BF16), vm((16, WIDTH), BF16), vm((WIDTH, 2 * C), BF16),
            vm((WIDTH, WIDTH), BF16), vm((WIDTH, 3 * C), BF16), vm((WIDTH, WIDTH), BF16), vm((WIDTH, 128), F32),
            vm((chunks, WIDTH, span), BF16), vm((chunks, WIDTH, span), F32), vm((chunks, WIDTH, span), F32),
            vm((chunks, 2 * C, span), F32), vm((chunks, WIDTH, span), F32), vm((chunks, C, span), BF16),
            vm((chunks, 8, span), F32), vm((chunks, 1, span), F32), vm((9 * C, WIDTH), F32), vm((9 * C, WIDTH), BF16),
            vm((80, 128), F32), vm((8, WIDTH), F32), vm((8, 8, 128), F32), vm((8, 8, 128), F32),
            pltpu.SemaphoreType.DMA((15,)), pltpu.SemaphoreType.DMA((8,)), pltpu.SemaphoreType.DMA((8,)),
            pltpu.SemaphoreType.DMA((8,)), pltpu.SemaphoreType.DMA((8,)),
        ],
        compiler_params=pltpu.CompilerParams(collective_id=0, has_side_effects=True, vmem_limit_bytes=56 * 1024 * 1024),
        name="layer",
    )(
        rel_vec, atom_feat, centre.reshape(16, 128), nbr_slot.reshape(16, 128), edge_mask.reshape(16, 128), send_rows, w_radial,
        w_centre, w_nbr, w_env.T, w_val.T, w_mix, w_scal, w_read, w_out.reshape(1, WIDTH),
    )
    return (energy.reshape(WIDTH), forces)


def solution(mesh):
    edges = P(("space", "grp"))
    placed = (
        P(None, ("space", "grp")), P(("space", "grp"), None), edges, edges, edges, P(("space", "grp"), None),
    ) + (P(),) * 9
    return jax.shard_map(
        functools.partial(per_device, mesh.shape["space"], mesh.shape["grp"]),
        mesh=mesh,
        in_specs=placed,
        out_specs=(edges, P(None, ("space", "grp"))),
        check_vma=False,
    )
```

```python
import functools
import math

import jax
import jax.numpy as jnp
from jax import lax
from jax.experimental import pallas as pl
from jax.experimental.pallas import tpu as pltpu
from jax.sharding import PartitionSpec as P

F32 = jnp.float32
BF16 = jnp.bfloat16
MESH = pl.DeviceIdType.MESH
OFFSETS = ((-1, -1), (-1, 0), (-1, 1), (0, -1), (0, 1), (1, -1), (1, 0), (1, 1))
STAGES = ((0, 1), (2, 3), (4, 5, 6, 7))
BACK = (0, 1, 3, 2, 5, 4, 7, 6)
CUTOFF = 5.0
R3, R5, R15 = math.sqrt(3.0), math.sqrt(5.0), math.sqrt(15.0)
DEGREES = ((0,), (1, 2, 3), (4, 5, 6, 7, 8))
WIDTH = 256
EDGES = 2048
C = 64


def mm(lhs, rhs):
    return jnp.dot(lhs, rhs, preferred_element_type=F32)


def mm_nt(lhs, rhs):
    return lax.dot_general(lhs, rhs, (((1,), (1,)), ((), ())), preferred_element_type=F32)


def turned(block):
    return block.astype(F32).T.astype(BF16)


def gated(half):
    rise = 1.0 + jnp.tanh(half)
    active = half * rise
    return active, (rise + active * (2.0 - rise)).astype(BF16)


def halved(block):
    return (0.5 * block.astype(F32)).astype(BF16)


def pipeline(steps):
    waiting, running = list(steps), []
    while waiting or running:
        if waiting:
            running.append(waiting.pop(0))
        running = [step for step in running if next(step, "end") != "end"]


def onehot(row, count, first=0):
    ids = lax.broadcasted_iota(jnp.int16, (count, row.shape[1]), 0)
    own = (row - first).astype(jnp.int16)
    return jnp.where(ids == own, jnp.bfloat16(1.0), jnp.bfloat16(0.0))


def down(block):
    return jnp.sum(block, axis=0, keepdims=True)


def part(block, i):
    return block[i * C : (i + 1) * C]


def scaled(block, harm):
    return block if harm is None else block * harm


def harmonics_exact(x, y, z):
    return [
        None, R3 * x, R3 * y, R3 * z,
        R15 * x * y, R15 * y * z, 0.5 * R5 * (3.0 * z * z - 1.0), R15 * x * z, 0.5 * R15 * (x * x - y * y),
    ]


def harmonics(x, y, z):
    return [None] + [harm.astype(BF16) for harm in harmonics_exact(x, y, z)[1:]]


def geometry(vec, centre, slot, mask, geo, dense):
    for i in range(3):
        for b in range(16):
            dense[i, b : b + 1, :] = vec[i : i + 1, b * 128 : (b + 1) * 128]
    real = mask[...] > 0
    vx, vy, vz = [jnp.where(real, dense[i], 1.0) for i in range(3)]
    dist = jnp.sqrt(vx * vx + vy * vy + vz * vz)
    inv = 1.0 / dist
    t = dist / CUTOFF
    angle = math.pi * t
    sin1, cos1 = jnp.sin(angle), jnp.cos(angle)
    scale = math.sqrt(2.0 / CUTOFF)
    sins, coss = [jnp.zeros_like(t), sin1], [jnp.ones_like(t), cos1]
    for n in range(2, 9):
        sins.append(2.0 * cos1 * sins[-1] - sins[-2])
        coss.append(2.0 * cos1 * coss[-1] - coss[-2])
    for n in range(1, 9):
        radial = scale * sins[n] * inv
        geo[0, :, n - 1, :] = radial
        geo[1, :, n - 1, :] = (scale * n * math.pi / CUTOFF * coss[n] - radial) * inv
    t2 = t * t
    t4 = t2 * t2
    t5, t6, t7, t8 = t4 * t, t4 * t2, t4 * t2 * t, t4 * t4
    geo[2, :, 0, :] = vx * inv
    geo[2, :, 1, :] = vy * inv
    geo[2, :, 2, :] = vz * inv
    geo[2, :, 3, :] = inv
    geo[2, :, 4, :] = 1.0 - 28.0 * t6 + 48.0 * t7 - 21.0 * t8
    geo[2, :, 5, :] = (336.0 * t6 - 168.0 * t5 - 168.0 * t7) / CUTOFF
    geo[2, :, 6, :] = jnp.where(real, centre[...], -1).astype(F32)
    geo[2, :, 7, :] = jnp.where(real, slot[...], -1).astype(F32)


def kernel(
    space, grp, span,
    vec_in, feat_in, centre_in, slot_in, mask_in, rows_in, w_radial_in, w_centre_in, w_nbr_in, w_env_in, w_val_in,
    w_mix_in, w_scal_in, w_read_in, w_out_in,
    result_ref, rest_ref,
    vec, feat, centre, slot, mask, send_rows, w_radial, w_centre, w_nbr, wevt, w_mix, w_scal, w_read, w_out,
    outgoing, tab, near, geo, dense, wr, wrhl, wev, wmixt, wreadt, wout, woutf,
    hot_s, far_s, lat_s, actb_s, act_s, slope_s, wv_s, back_s, vbar_s, hbar_s, en_s, env_s, envh_s, fsum, leaving, landed,
    in_sem, send_sem, recv_sem, send_sem2, recv_sem2,
):
    wide = span // 128
    chunks = EDGES // span
    me_s, me_g = lax.axis_index("space"), lax.axis_index("grp")
    peers = [(lax.rem(me_s + a + space, space), lax.rem(me_g + b + grp, grp)) for a, b in OFFSETS]
    barrier = pltpu.get_barrier_semaphore()
    for peer in peers:
        pl.semaphore_signal(barrier, inc=1, device_id=peer, device_id_type=MESH)
    pairs = [
        (feat_in, feat), (w_nbr_in, w_nbr), (rows_in, send_rows), (w_centre_in, w_centre), (vec_in, vec), (centre_in, centre),
        (slot_in, slot), (mask_in, mask), (w_radial_in, w_radial), (w_env_in, wevt.at[0:C]), (w_val_in, wevt.at[C : 2 * C]),
        (w_mix_in, w_mix), (w_scal_in, w_scal), (w_read_in, w_read), (w_out_in, w_out),
    ]
    loads = [pltpu.make_async_copy(a, b, in_sem.at[i]) for i, (a, b) in enumerate(pairs)]
    for load in loads:
        load.start()
    for load in loads[:3]:
        load.wait()
    own = (0.5 * mm(feat[...], w_nbr[...])).T.astype(BF16)
    near[:, 0:WIDTH] = own
    outgoing[...] = mm(own, onehot(send_rows[...], WIDTH)).astype(BF16)
    pl.semaphore_wait(barrier, 8)

    mate = 1 - 2 * lax.rem(me_g, 2)
    steps = ((0, mate), (0, -mate), (-1, 0), (1, 0), (-1, mate), (1, mate), (-1, -mate), (1, -mate))
    partners = [(lax.rem(me_s + a + space, space), lax.rem(me_g + b + grp, grp)) for a, b in steps]
    flat = [3 * (a + 1) + b + 1 for a, b in steps]
    blocks = [f - jnp.where(f > 4, 1, 0) for f in flat]

    def remote(source, target, sends, receives, device):
        return pltpu.make_async_remote_copy(
            src_ref=source, dst_ref=target, send_sem=sends, recv_sem=receives, device_id=device, device_id_type=MESH
        )

    def sent(role):
        return remote(outgoing, tab.at[BACK[role]], send_sem.at[role], recv_sem.at[BACK[role]], partners[role])

    def passed(role):
        return remote(tab.at[role - 2], tab.at[role], send_sem.at[role], recv_sem.at[role], partners[0])

    copies = {role: sent(role) for role in (3, 2, 7, 6, 1, 0)}
    for role in (3, 2, 7, 6, 1, 0):
        copies[role].start()
    for load in loads[3:]:
        load.wait()
    near[:, WIDTH:] = (0.5 * mm(feat[...], w_centre[...])).T.astype(BF16)
    geometry(vec, centre, slot, mask, geo, dense)
    half_radial = 0.5 * w_radial[...]
    high = half_radial.astype(BF16).astype(F32)
    low = half_radial - high
    stacked = jnp.concatenate([high, low, high, jnp.zeros((104, WIDTH), F32)], axis=0)
    wr[...] = stacked.T[:, :32].astype(BF16)
    wrhl[...] = jnp.concatenate([high, low], axis=0).astype(BF16)

    def rows(group, j):
        return jnp.concatenate([geo[group, wide * j + i] for i in range(wide)], axis=1)

    def fields(j):
        block = rows(2, j)
        return [block[i : i + 1] for i in range(8)]

    def index(row):
        return row.astype(jnp.int32)

    for j in range(chunks):
        radial = rows(0, j)
        top = radial.astype(BF16).astype(F32)
        terms = jnp.concatenate([top, top, radial - top, jnp.zeros_like(top)], axis=0).astype(BF16)
        marks = fields(j)
        hot_s[j] = onehot(index(marks[6]), WIDTH)
        hot = jnp.concatenate([onehot(index(marks[7]), WIDTH), hot_s[j]], axis=0)
        act_s[j] = mm(near[...], hot) + mm(wr[...], terms)

    wev[...] = turned(wevt[...])
    w_mix[...] = halved(w_mix[...])
    w_scal[...] = halved(w_scal[...])
    w_read[...] = halved(w_read[...])
    wmixt[:, 0:WIDTH] = turned(w_mix[...])
    padded = jnp.concatenate([w_scal[...].astype(F32), jnp.zeros((C, WIDTH), F32)], axis=0)
    wmixt[:, WIDTH:] = padded.T.astype(BF16)
    wreadt[...] = turned(w_read[...])
    woutf[...] = jnp.broadcast_to(w_out[...], (128, WIDTH)).T
    wout[...] = woutf[...].astype(BF16)
    for j in range(chunks):
        slots = index(fields(j)[7])
        far_s[j] = jnp.concatenate([onehot(slots, 128, WIDTH + 128 * c) for c in blocks], axis=0)

    def add(total, term, j):
        total[...] = term if j == 0 else total[...] + term

    def gathered(j, stage):
        hot = far_s[j, 128 * stage[0] : 128 * (stage[-1] + 1)]
        return act_s[j] + mm(jnp.concatenate([tab[role] for role in stage], axis=1), hot)

    for role in (2, 3):
        copies[BACK[role]].wait_recv()
        copies[role + 2] = passed(role + 2)
        copies[role + 2].start()
    for role in (0, 1):
        copies[role].wait_recv()
    for stage in STAGES[:2]:
        for j in range(chunks):
            act_s[j] = gathered(j, stage)
    for role in (4, 5):
        copies[role].wait_recv()
    for role in (6, 7):
        copies[BACK[role]].wait_recv()

    def forward(j):
        x, y, z, _, envelope, _, _, _ = fields(j)
        lifted = gathered(j, STAGES[2])
        yield
        active, slope = gated(lifted)
        actb_s[j] = active.astype(BF16)
        slope_s[j] = slope
        latent = (active * envelope).astype(BF16)
        lat_s[j, 0:WIDTH] = latent
        yield
        wv = mm(wevt[...], latent).astype(BF16)
        wv_s[j] = wv
        yield
        weights = wv[:C]
        harm = harmonics(x, y, z)
        spread = jnp.concatenate([scaled(weights, harm[i]) for i in range(9)], axis=0)
        yield
        add(env_s, mm_nt(spread, hot_s[j]), j)

    def middle(j):
        x, y, z, _, _, _, _, _ = fields(j)
        hot = hot_s[j]
        exact, harm = harmonics_exact(x, y, z), harmonics(x, y, z)
        local = mm(envh_s[...], hot)
        yield
        values = wv_s[j, C:]
        invariants = []
        for degree in DEGREES:
            whole = None
            for i in degree:
                term = scaled(part(local, i), exact[i])
                whole = term if whole is None else whole + term
            invariants.append(whole.astype(BF16))
        lat_s[j, WIDTH:] = jnp.concatenate([q * values for q in invariants] + [jnp.zeros_like(values)], axis=0)
        yield
        update = mm(wmixt[...], lat_s[j])
        yield
        active, slope = gated(update)
        mixed = lat_s[j, 0:WIDTH] + active.astype(BF16)
        yield
        hidden = mm(wreadt[...], mixed)
        yield
        active_h, slope_h = gated(hidden)
        en_s[j] = down(active_h * jnp.concatenate([woutf[...]] * wide, axis=1))
        hidden_bar = jnp.concatenate([wout[...]] * wide, axis=1) * slope_h
        yield
        mixed_bar = mm(w_read[...], hidden_bar)
        yield
        mixed_bar = mixed_bar.astype(BF16)
        update_bar = mixed_bar * slope
        yield
        back_s[j] = mixed_bar.astype(F32) + mm(w_mix[...], update_bar)
        scal_f = mm(w_scal[...], update_bar)
        scal_bar = scal_f.astype(BF16)
        yield
        values_bar = None
        locals_bar, products = [], []
        for level, degree in enumerate(DEGREES):
            bar = part(scal_bar, level)
            term = bar * invariants[level]
            values_bar = term if values_bar is None else values_bar + term
            inner_f = part(scal_f, level) * values.astype(F32)
            inner = inner_f.astype(BF16)
            for i in degree:
                locals_bar.append(scaled(inner, harm[i]))
                if i:
                    products.append(down(part(local, i) * inner_f))
        vbar_s[j] = values_bar
        hbar_s[j] = jnp.concatenate(products, axis=0)
        yield
        add(env_s, mm_nt(jnp.concatenate(locals_bar, axis=0), hot), j)

    def backward(j):
        x, y, z, inv, envelope, slope_env, centres, slots = fields(j)
        slots, centres = index(slots), index(centres)
        hot = hot_s[j]
        harm = harmonics_exact(x, y, z)
        spread_bar = mm(envh_s[...], hot)
        yield
        weights = wv_s[j, :C].astype(F32)
        weights_bar = part(spread_bar, 0)
        for i in range(1, 9):
            weights_bar = weights_bar + part(spread_bar, i) * harm[i]
        products = [down(part(spread_bar, i) * weights) for i in range(1, 9)]
        wv_bar = jnp.concatenate([weights_bar.astype(BF16), vbar_s[j]], axis=0)
        yield
        latent_f = back_s[j] + mm(wev[...], wv_bar)
        latent_bar = latent_f.astype(BF16)
        harm_bar = hbar_s[j] + jnp.concatenate(products, axis=0)
        bars = [None] + [harm_bar[i : i + 1] for i in range(8)]
        yield
        envelope_bar = down(latent_f * actb_s[j].astype(F32))
        lifted_bar = latent_bar * envelope.astype(BF16) * slope_s[j]
        yield
        radial_bar = mm(wrhl[...], lifted_bar)
        yield
        dist_bar = down((radial_bar[:8] + radial_bar[8:]) * rows(1, j)) + envelope_bar * slope_env
        ux = R3 * bars[1] + R15 * (y * bars[4] + z * bars[7] + x * bars[8])
        uy = R3 * bars[2] + R15 * (x * bars[4] + z * bars[5] - y * bars[8])
        uz = R3 * bars[3] + R15 * (y * bars[5] + x * bars[7]) + 3.0 * R5 * z * bars[6]
        along = dist_bar - (x * ux + y * uy + z * uz) * inv
        grads = jnp.concatenate([ux * inv + x * along, uy * inv + y * along, uz * inv + z * along, en_s[j]], axis=0)
        top = grads.astype(BF16).astype(F32)
        both = jnp.concatenate([top, grads - top], axis=0)
        split = [jnp.where(lax.shift_right_arithmetic(slots, 7) == h, both, 0.0) for h in range(10)]
        split += [jnp.where(lax.shift_right_arithmetic(centres, 7) == h, both, 0.0) for h in range(2)]
        low = jnp.concatenate([onehot(lax.bitwise_and(row, 127), 128) for row in (slots, centres)], axis=0)
        yield
        add(fsum, mm_nt(jnp.concatenate(split, axis=0).astype(BF16), low), j)

    pipeline(forward(j) for j in range(chunks))
    envh_s[...] = (env_s[...] * 0.125).astype(BF16)
    pipeline(middle(j) for j in range(chunks))
    envh_s[...] = (env_s[...] * 0.125).astype(BF16)
    pipeline(backward(j) for j in range(chunks))

    def summed(first, side):
        return fsum[first : first + 4, 128 * side : 128 * side + 128] + fsum[first + 4 : first + 8, 128 * side : 128 * side + 128]

    for c in range(8):
        leaving[c, 0:4] = summed(16 + 8 * c, 0)
        leaving[c, 4:8] = jnp.zeros((4, 128), F32)
    returns = [remote(leaving.at[c], landed.at[7 - c], send_sem2.at[c], recv_sem2.at[7 - c], peers[c]) for c in range(8)]
    for c in (0, 2, 5, 7, 1, 6, 3, 4):
        returns[c].start()
    centre_sum = jnp.concatenate([summed(80, 1), summed(88, 1)], axis=1)
    own_sum = jnp.concatenate([summed(0, 0), summed(8, 0)], axis=1)
    hot = onehot(send_rows[...], WIDTH)
    for copy in returns:
        copy.wait_recv()
    total = landed[0]
    for c in range(1, 8):
        total = total + landed[c]
    top = total.astype(BF16).astype(F32)
    away = mm_nt(jnp.concatenate([top, total - top], axis=0).astype(BF16), hot)
    result_ref[...] = centre_sum
    rest_ref[0:3] = -own_sum[0:3] - (away[0:3] + away[8:11])
    rest_ref[3:4] = jnp.zeros((1, WIDTH), F32)
    for copy in list(copies.values()) + returns:
        copy.wait_send()


def per_device(
    space, grp,
    rel_vec, atom_feat, centre, nbr_slot, edge_mask, send_rows, w_radial, w_centre, w_nbr, w_env, w_val, w_mix, w_scal,
    w_read, w_out,
):
    span = 512
    chunks = EDGES // span
    shape = jax.ShapeDtypeStruct
    vm = pltpu.VMEM
    result = pl.pallas_call(
        functools.partial(kernel, space, grp, span),
        out_shape=[vm((4, WIDTH), F32)] * 2,
        in_specs=[pl.BlockSpec(memory_space=pl.ANY)] * 15,
        out_specs=[pl.BlockSpec(memory_space=pltpu.VMEM)] * 2,
        scratch_shapes=[
            vm((3, EDGES), F32), vm((WIDTH, WIDTH), BF16), vm((16, 128), jnp.int32), vm((16, 128), jnp.int32),
            vm((16, 128), jnp.int32), vm((1, 128), jnp.int32), vm((8, WIDTH), F32), vm((WIDTH, WIDTH), BF16),
            vm((WIDTH, WIDTH), BF16), vm((2 * C, WIDTH), BF16), vm((WIDTH, WIDTH), BF16), vm((3 * C, WIDTH), BF16),
            vm((WIDTH, WIDTH), BF16), vm((1, WIDTH), F32),
            vm((WIDTH, 128), BF16), vm((8, WIDTH, 128), BF16), vm((WIDTH, 2 * WIDTH), BF16), vm((3, 16, 8, 128), F32),
            vm((3, 16, 128), F32), vm((WIDTH, 32), BF16), vm((16, WIDTH), BF16), vm((WIDTH, 2 * C), BF16),
            vm((WIDTH, 2 * WIDTH), BF16), vm((WIDTH, WIDTH), BF16), vm((WIDTH, 128), BF16), vm((WIDTH, 128), F32),
            vm((chunks, WIDTH, span), BF16), vm((chunks, 8 * 128, span), BF16),
            vm((chunks, 2 * WIDTH, span), BF16), vm((chunks, WIDTH, span), BF16), vm((chunks, WIDTH, span), F32),
            vm((chunks, WIDTH, span), BF16), vm((chunks, 2 * C, span), BF16), vm((chunks, WIDTH, span), F32),
            vm((chunks, C, span), BF16), vm((chunks, 8, span), F32), vm((chunks, 1, span), F32), vm((9 * C, WIDTH), F32),
            vm((9 * C, WIDTH), BF16),
            vm((96, WIDTH), F32), vm((8, 8, 128), F32), vm((8, 8, 128), F32),
            pltpu.SemaphoreType.DMA((15,)), pltpu.SemaphoreType.DMA((8,)), pltpu.SemaphoreType.DMA((8,)),
            pltpu.SemaphoreType.DMA((8,)), pltpu.SemaphoreType.DMA((8,)),
        ],
        compiler_params=pltpu.CompilerParams(collective_id=0, has_side_effects=True, vmem_limit_bytes=56 * 1024 * 1024),
        name="layer",
    )(
        rel_vec, atom_feat, centre.reshape(16, 128), nbr_slot.reshape(16, 128), edge_mask.reshape(16, 128), send_rows, w_radial,
        w_centre, w_nbr, w_env.T, w_val.T, w_mix, w_scal, w_read, w_out.reshape(1, WIDTH),
    )
    total = result[0] + result[1]
    return (total[3], total[0:3])


def solution(mesh):
    edges = P(("space", "grp"))
    placed = (
        P(None, ("space", "grp")), P(("space", "grp"), None), edges, edges, edges, P(("space", "grp"), None),
    ) + (P(),) * 9
    return jax.shard_map(
        functools.partial(per_device, mesh.shape["space"], mesh.shape["grp"]),
        mesh=mesh,
        in_specs=placed,
        out_specs=(edges, P(None, ("space", "grp"))),
        check_vma=False,
    )
```

```python
import functools
import math

import jax
import jax.numpy as jnp
from jax import lax
from jax.experimental import pallas as pl
from jax.experimental.pallas import tpu as pltpu
from jax.sharding import PartitionSpec as P

F32 = jnp.float32
BF16 = jnp.bfloat16
MESH = pl.DeviceIdType.MESH
OFFSETS = ((-1, -1), (-1, 0), (-1, 1), (0, -1), (0, 1), (1, -1), (1, 0), (1, 1))
STAGES = ((0, 1, 2, 3), (4, 5, 6, 7))
ORDER = (2, 3, 6, 7, 0, 1)
BACK = (0, 1, 3, 2, 5, 4, 7, 6)
CUTOFF = 5.0
R3, R5, R15 = math.sqrt(3.0), math.sqrt(5.0), math.sqrt(15.0)
DEGREES = ((0,), (1, 2, 3), (4, 5, 6, 7, 8))
WIDTH = 256
EDGES = 2048
C = 64


def mm(lhs, rhs):
    return jnp.dot(lhs, rhs, preferred_element_type=F32)


def mm_nt(lhs, rhs):
    return lax.dot_general(lhs, rhs, (((1,), (1,)), ((), ())), preferred_element_type=F32)


def turned(block):
    return block.astype(F32).T.astype(BF16)


def gated(half):
    rise = 1.0 + jnp.tanh(half)
    active = half * rise
    return active, (rise + active * (2.0 - rise)).astype(BF16)


def halved(block):
    return (0.5 * block.astype(F32)).astype(BF16)


def pipeline(steps):
    waiting, running = list(steps), []
    while waiting or running:
        if waiting:
            running.append(waiting.pop(0))
        running = [step for step in running if next(step, "end") != "end"]


def onehot(row, count, first=0):
    ids = lax.broadcasted_iota(jnp.int16, (count, row.shape[1]), 0)
    own = (row - first).astype(jnp.int16)
    return jnp.where(ids == own, jnp.bfloat16(1.0), jnp.bfloat16(0.0))


def down(block):
    return jnp.sum(block, axis=0, keepdims=True)


def part(block, i):
    return block[i * C : (i + 1) * C]


def scaled(block, harm):
    return block if harm is None else block * harm


def harmonics(x, y, z):
    return [
        None, R3 * x, R3 * y, R3 * z,
        R15 * x * y, R15 * y * z, 0.5 * R5 * (3.0 * z * z - 1.0), R15 * x * z, 0.5 * R15 * (x * x - y * y),
    ]


def geometry(vec, centre, slot, mask, geo, dense):
    for i in range(3):
        for b in range(16):
            dense[i, b : b + 1, :] = vec[i : i + 1, b * 128 : (b + 1) * 128]
    real = mask[...] > 0
    vx, vy, vz = [jnp.where(real, dense[i], 1.0) for i in range(3)]
    dist = jnp.sqrt(vx * vx + vy * vy + vz * vz)
    inv = 1.0 / dist
    t = dist / CUTOFF
    angle = math.pi * t
    sin1, cos1 = jnp.sin(angle), jnp.cos(angle)
    scale = math.sqrt(2.0 / CUTOFF)
    sins, coss = [jnp.zeros_like(t), sin1], [jnp.ones_like(t), cos1]
    for n in range(2, 9):
        sins.append(2.0 * cos1 * sins[-1] - sins[-2])
        coss.append(2.0 * cos1 * coss[-1] - coss[-2])
    for n in range(1, 9):
        radial = scale * sins[n] * inv
        geo[0, :, n - 1, :] = radial
        geo[1, :, n - 1, :] = (scale * n * math.pi / CUTOFF * coss[n] - radial) * inv
    t2 = t * t
    t4 = t2 * t2
    t5, t6, t7, t8 = t4 * t, t4 * t2, t4 * t2 * t, t4 * t4
    geo[2, :, 0, :] = vx * inv
    geo[2, :, 1, :] = vy * inv
    geo[2, :, 2, :] = vz * inv
    geo[2, :, 3, :] = inv
    geo[2, :, 4, :] = 1.0 - 28.0 * t6 + 48.0 * t7 - 21.0 * t8
    geo[2, :, 5, :] = (336.0 * t6 - 168.0 * t5 - 168.0 * t7) / CUTOFF
    geo[2, :, 6, :] = jnp.where(real, centre[...], -1).astype(F32)
    geo[2, :, 7, :] = jnp.where(real, slot[...], -1).astype(F32)


def kernel(
    space, grp, span,
    vec_in, feat_in, centre_in, slot_in, mask_in, rows_in, w_radial_in, w_centre_in, w_nbr_in, w_env_in, w_val_in,
    w_mix_in, w_scal_in, w_read_in, w_out_in,
    result_ref, rest_ref,
    vec, feat, centre, slot, mask, send_rows, w_radial, w_centre, w_nbr, wevt, w_mix, w_scal, w_read, w_out,
    outgoing, tab, near, geo, dense, wr, wrhl, wev, wmixt, wreadt, wout, woutf,
    hot_s, far_s, lat_s, actb_s, act_s, slope_s, wv_s, back_s, vbar_s, hbar_s, en_s, env_s, envh_s, fsum, leaving, landed,
    in_sem, send_sem, recv_sem, send_sem2, recv_sem2,
):
    wide = span // 128
    chunks = EDGES // span
    me_s, me_g = lax.axis_index("space"), lax.axis_index("grp")
    peers = [(lax.rem(me_s + a + space, space), lax.rem(me_g + b + grp, grp)) for a, b in OFFSETS]
    barrier = pltpu.get_barrier_semaphore()
    for peer in peers:
        pl.semaphore_signal(barrier, inc=1, device_id=peer, device_id_type=MESH)
    pairs = [
        (feat_in, feat), (w_nbr_in, w_nbr), (rows_in, send_rows), (w_centre_in, w_centre), (vec_in, vec), (centre_in, centre),
        (slot_in, slot), (mask_in, mask), (w_radial_in, w_radial), (w_env_in, wevt.at[0:C]), (w_val_in, wevt.at[C : 2 * C]),
        (w_mix_in, w_mix), (w_scal_in, w_scal), (w_read_in, w_read), (w_out_in, w_out),
    ]
    loads = [pltpu.make_async_copy(a, b, in_sem.at[i]) for i, (a, b) in enumerate(pairs)]
    for load in loads:
        load.start()
    for load in loads[:3]:
        load.wait()
    own = (0.5 * mm(feat[...], w_nbr[...])).T.astype(BF16)
    near[:, 0:WIDTH] = own
    outgoing[...] = mm(own, onehot(send_rows[...], WIDTH)).astype(BF16)
    pl.semaphore_wait(barrier, 8)

    mate = 1 - 2 * lax.rem(me_g, 2)
    steps = ((0, mate), (0, -mate), (-1, 0), (1, 0), (-1, mate), (1, mate), (-1, -mate), (1, -mate))
    partners = [(lax.rem(me_s + a + space, space), lax.rem(me_g + b + grp, grp)) for a, b in steps]
    flat = [3 * (a + 1) + b + 1 for a, b in steps]
    blocks = [f - jnp.where(f > 4, 1, 0) for f in flat]

    def remote(source, target, sends, receives, device):
        return pltpu.make_async_remote_copy(
            src_ref=source, dst_ref=target, send_sem=sends, recv_sem=receives, device_id=device, device_id_type=MESH
        )

    def sent(role):
        return remote(outgoing, tab.at[BACK[role]], send_sem.at[role], recv_sem.at[BACK[role]], partners[role])

    def passed(role):
        return remote(tab.at[role - 2], tab.at[role], send_sem.at[role], recv_sem.at[role], partners[0])

    copies = {role: sent(role) for role in ORDER}
    for role in ORDER:
        copies[role].start()
    for load in loads[3:]:
        load.wait()
    near[:, WIDTH:] = (0.5 * mm(feat[...], w_centre[...])).T.astype(BF16)
    geometry(vec, centre, slot, mask, geo, dense)
    half_radial = 0.5 * w_radial[...]
    high = half_radial.astype(BF16).astype(F32)
    low = half_radial - high
    stacked = jnp.concatenate([high, low, high, jnp.zeros((104, WIDTH), F32)], axis=0)
    wr[...] = stacked.T[:, :32].astype(BF16)
    wrhl[...] = jnp.concatenate([high, low], axis=0).astype(BF16)

    def rows(group, j):
        return jnp.concatenate([geo[group, wide * j + i] for i in range(wide)], axis=1)

    def fields(j):
        block = rows(2, j)
        return [block[i : i + 1] for i in range(8)]

    def index(row):
        return row.astype(jnp.int32)

    for j in range(chunks):
        radial = rows(0, j)
        top = radial.astype(BF16).astype(F32)
        terms = jnp.concatenate([top, top, radial - top, jnp.zeros_like(top)], axis=0).astype(BF16)
        marks = fields(j)
        hot_s[j] = onehot(index(marks[6]), WIDTH)
        hot = jnp.concatenate([onehot(index(marks[7]), WIDTH), hot_s[j]], axis=0)
        act_s[j] = mm(near[...], hot) + mm(wr[...], terms)

    wev[...] = turned(wevt[...])
    w_mix[...] = halved(w_mix[...])
    w_scal[...] = halved(w_scal[...])
    w_read[...] = halved(w_read[...])
    wmixt[:, 0:WIDTH] = turned(w_mix[...])
    padded = jnp.concatenate([w_scal[...].astype(F32), jnp.zeros((C, WIDTH), F32)], axis=0)
    wmixt[:, WIDTH:] = padded.T.astype(BF16)
    wreadt[...] = turned(w_read[...])
    woutf[...] = jnp.broadcast_to(w_out[...], (128, WIDTH)).T
    wout[...] = woutf[...].astype(BF16)
    for j in range(chunks):
        slots = index(fields(j)[7])
        far_s[j] = jnp.concatenate([onehot(slots, 128, WIDTH + 128 * c) for c in blocks], axis=0)

    def add(total, term, j):
        total[...] = term if j == 0 else total[...] + term

    def gathered(j, stage):
        hot = far_s[j, 128 * stage[0] : 128 * (stage[-1] + 1)]
        return act_s[j] + mm(jnp.concatenate([tab[role] for role in stage], axis=1), hot)

    for role in (2, 3):
        copies[BACK[role]].wait_recv()
        copies[role + 2] = passed(role + 2)
        copies[role + 2].start()
    for role in (0, 1):
        copies[role].wait_recv()
    for j in range(chunks):
        act_s[j] = gathered(j, STAGES[0])
    for role in (4, 5):
        copies[role].wait_recv()
    for role in (6, 7):
        copies[BACK[role]].wait_recv()

    def forward(j):
        x, y, z, _, envelope, _, _, _ = fields(j)
        lifted = gathered(j, STAGES[1])
        yield
        active, slope = gated(lifted)
        actb_s[j] = active.astype(BF16)
        slope_s[j] = slope
        latent = (active * envelope).astype(BF16)
        lat_s[j, 0:WIDTH] = latent
        yield
        wv = mm(wevt[...], latent)
        wv_s[j] = wv.astype(BF16)
        yield
        weights = wv[:C]
        harm = harmonics(x, y, z)
        spread = jnp.concatenate([scaled(weights, harm[i]).astype(BF16) for i in range(9)], axis=0)
        yield
        add(env_s, mm_nt(spread, hot_s[j]), j)

    def middle(j):
        x, y, z, _, _, _, _, _ = fields(j)
        hot = hot_s[j]
        harm = harmonics(x, y, z)
        local = mm(envh_s[...], hot)
        yield
        values = wv_s[j, C:]
        invariants = []
        for degree in DEGREES:
            whole = None
            for i in degree:
                term = scaled(part(local, i), harm[i])
                whole = term if whole is None else whole + term
            invariants.append(whole.astype(BF16))
        lat_s[j, WIDTH:] = jnp.concatenate([q * values for q in invariants] + [jnp.zeros_like(values)], axis=0)
        yield
        update = mm(wmixt[...], lat_s[j])
        yield
        active, slope = gated(update)
        mixed = lat_s[j, 0:WIDTH] + active.astype(BF16)
        yield
        hidden = mm(wreadt[...], mixed)
        yield
        active_h, slope_h = gated(hidden)
        en_s[j] = down(active_h * jnp.concatenate([woutf[...]] * wide, axis=1))
        hidden_bar = jnp.concatenate([wout[...]] * wide, axis=1) * slope_h
        yield
        mixed_bar = mm(w_read[...], hidden_bar)
        yield
        mixed_bar = mixed_bar.astype(BF16)
        update_bar = mixed_bar * slope
        yield
        back_s[j] = mixed_bar.astype(F32) + mm(w_mix[...], update_bar)
        scal_f = mm(w_scal[...], update_bar)
        scal_bar = scal_f.astype(BF16)
        yield
        values_bar = None
        locals_bar, products = [], []
        for level, degree in enumerate(DEGREES):
            bar = part(scal_bar, level)
            term = bar * invariants[level]
            values_bar = term if values_bar is None else values_bar + term
            inner = part(scal_f, level) * values.astype(F32)
            for i in degree:
                locals_bar.append(scaled(inner, harm[i]).astype(BF16))
                if i:
                    products.append(down(part(local, i) * inner))
        vbar_s[j] = values_bar
        hbar_s[j] = jnp.concatenate(products, axis=0)
        yield
        add(env_s, mm_nt(jnp.concatenate(locals_bar, axis=0), hot), j)

    def backward(j):
        x, y, z, inv, envelope, slope_env, centres, slots = fields(j)
        slots, centres = index(slots), index(centres)
        hot = hot_s[j]
        harm = harmonics(x, y, z)
        spread_bar = mm(envh_s[...], hot)
        yield
        weights = wv_s[j, :C].astype(F32)
        weights_bar = part(spread_bar, 0)
        for i in range(1, 9):
            weights_bar = weights_bar + part(spread_bar, i) * harm[i]
        products = [down(part(spread_bar, i) * weights) for i in range(1, 9)]
        wv_bar = jnp.concatenate([weights_bar.astype(BF16), vbar_s[j]], axis=0)
        yield
        latent_f = back_s[j] + mm(wev[...], wv_bar)
        latent_bar = latent_f.astype(BF16)
        harm_bar = hbar_s[j] + jnp.concatenate(products, axis=0)
        bars = [None] + [harm_bar[i : i + 1] for i in range(8)]
        yield
        envelope_bar = down(latent_f * actb_s[j].astype(F32))
        lifted_bar = latent_bar * envelope.astype(BF16) * slope_s[j]
        yield
        radial_bar = mm(wrhl[...], lifted_bar)
        yield
        dist_bar = down((radial_bar[:8] + radial_bar[8:]) * rows(1, j)) + envelope_bar * slope_env
        ux = R3 * bars[1] + R15 * (y * bars[4] + z * bars[7] + x * bars[8])
        uy = R3 * bars[2] + R15 * (x * bars[4] + z * bars[5] - y * bars[8])
        uz = R3 * bars[3] + R15 * (y * bars[5] + x * bars[7]) + 3.0 * R5 * z * bars[6]
        along = dist_bar - (x * ux + y * uy + z * uz) * inv
        grads = jnp.concatenate([ux * inv + x * along, uy * inv + y * along, uz * inv + z * along, en_s[j]], axis=0)
        top = grads.astype(BF16).astype(F32)
        both = jnp.concatenate([top, grads - top], axis=0)
        split = [jnp.where(lax.shift_right_arithmetic(slots, 7) == h, both, 0.0) for h in range(10)]
        split += [jnp.where(lax.shift_right_arithmetic(centres, 7) == h, both, 0.0) for h in range(2)]
        low = jnp.concatenate([onehot(lax.bitwise_and(row, 127), 128) for row in (slots, centres)], axis=0)
        yield
        add(fsum, mm_nt(jnp.concatenate(split, axis=0).astype(BF16), low), j)

    pipeline(forward(j) for j in range(chunks))
    envh_s[...] = (env_s[...] * 0.125).astype(BF16)
    pipeline(middle(j) for j in range(chunks))
    envh_s[...] = (env_s[...] * 0.125).astype(BF16)
    pipeline(backward(j) for j in range(chunks))

    def summed(first, side):
        return fsum[first : first + 4, 128 * side : 128 * side + 128] + fsum[first + 4 : first + 8, 128 * side : 128 * side + 128]

    for c in range(8):
        leaving[c, 0:4] = summed(16 + 8 * c, 0)
        leaving[c, 4:8] = jnp.zeros((4, 128), F32)
    returns = [remote(leaving.at[c], landed.at[7 - c], send_sem2.at[c], recv_sem2.at[7 - c], peers[c]) for c in range(8)]
    for c in (0, 2, 5, 7, 1, 6, 3, 4):
        returns[c].start()
    centre_sum = jnp.concatenate([summed(80, 1), summed(88, 1)], axis=1)
    own_sum = jnp.concatenate([summed(0, 0), summed(8, 0)], axis=1)
    hot = onehot(send_rows[...], WIDTH)
    for copy in returns:
        copy.wait_recv()
    total = landed[0]
    for c in range(1, 8):
        total = total + landed[c]
    top = total.astype(BF16).astype(F32)
    away = mm_nt(jnp.concatenate([top, total - top], axis=0).astype(BF16), hot)
    result_ref[...] = centre_sum
    rest_ref[0:3] = -own_sum[0:3] - (away[0:3] + away[8:11])
    rest_ref[3:4] = jnp.zeros((1, WIDTH), F32)
    for copy in list(copies.values()) + returns:
        copy.wait_send()


def per_device(
    space, grp,
    rel_vec, atom_feat, centre, nbr_slot, edge_mask, send_rows, w_radial, w_centre, w_nbr, w_env, w_val, w_mix, w_scal,
    w_read, w_out,
):
    span = 512
    chunks = EDGES // span
    shape = jax.ShapeDtypeStruct
    vm = pltpu.VMEM
    result = pl.pallas_call(
        functools.partial(kernel, space, grp, span),
        out_shape=[vm((4, WIDTH), F32)] * 2,
        in_specs=[pl.BlockSpec(memory_space=pl.ANY)] * 15,
        out_specs=[pl.BlockSpec(memory_space=pltpu.VMEM)] * 2,
        scratch_shapes=[
            vm((3, EDGES), F32), vm((WIDTH, WIDTH), BF16), vm((16, 128), jnp.int32), vm((16, 128), jnp.int32),
            vm((16, 128), jnp.int32), vm((1, 128), jnp.int32), vm((8, WIDTH), F32), vm((WIDTH, WIDTH), BF16),
            vm((WIDTH, WIDTH), BF16), vm((2 * C, WIDTH), BF16), vm((WIDTH, WIDTH), BF16), vm((3 * C, WIDTH), BF16),
            vm((WIDTH, WIDTH), BF16), vm((1, WIDTH), F32),
            vm((WIDTH, 128), BF16), vm((8, WIDTH, 128), BF16), vm((WIDTH, 2 * WIDTH), BF16), vm((3, 16, 8, 128), F32),
            vm((3, 16, 128), F32), vm((WIDTH, 32), BF16), vm((16, WIDTH), BF16), vm((WIDTH, 2 * C), BF16),
            vm((WIDTH, 2 * WIDTH), BF16), vm((WIDTH, WIDTH), BF16), vm((WIDTH, 128), BF16), vm((WIDTH, 128), F32),
            vm((chunks, WIDTH, span), BF16), vm((chunks, 8 * 128, span), BF16),
            vm((chunks, 2 * WIDTH, span), BF16), vm((chunks, WIDTH, span), BF16), vm((chunks, WIDTH, span), F32),
            vm((chunks, WIDTH, span), BF16), vm((chunks, 2 * C, span), BF16), vm((chunks, WIDTH, span), F32),
            vm((chunks, C, span), BF16), vm((chunks, 8, span), F32), vm((chunks, 1, span), F32), vm((9 * C, WIDTH), F32),
            vm((9 * C, WIDTH), BF16),
            vm((96, WIDTH), F32), vm((8, 8, 128), F32), vm((8, 8, 128), F32),
            pltpu.SemaphoreType.DMA((15,)), pltpu.SemaphoreType.DMA((8,)), pltpu.SemaphoreType.DMA((8,)),
            pltpu.SemaphoreType.DMA((8,)), pltpu.SemaphoreType.DMA((8,)),
        ],
        compiler_params=pltpu.CompilerParams(collective_id=0, has_side_effects=True, vmem_limit_bytes=56 * 1024 * 1024),
        name="layer",
    )(
        rel_vec, atom_feat, centre.reshape(16, 128), nbr_slot.reshape(16, 128), edge_mask.reshape(16, 128), send_rows, w_radial,
        w_centre, w_nbr, w_env.T, w_val.T, w_mix, w_scal, w_read, w_out.reshape(1, WIDTH),
    )
    total = result[0] + result[1]
    return (total[3], total[0:3])


def solution(mesh):
    edges = P(("space", "grp"))
    placed = (
        P(None, ("space", "grp")), P(("space", "grp"), None), edges, edges, edges, P(("space", "grp"), None),
    ) + (P(),) * 9
    return jax.shard_map(
        functools.partial(per_device, mesh.shape["space"], mesh.shape["grp"]),
        mesh=mesh,
        in_specs=placed,
        out_specs=(edges, P(None, ("space", "grp"))),
        check_vma=False,
    )
```

```python
import functools
import math

import jax
import jax.numpy as jnp
from jax import lax
from jax.experimental import pallas as pl
from jax.experimental.pallas import tpu as pltpu
from jax.sharding import PartitionSpec as P

F32 = jnp.float32
BF16 = jnp.bfloat16
MESH = pl.DeviceIdType.MESH
OFFSETS = ((-1, -1), (-1, 0), (-1, 1), (0, -1), (0, 1), (1, -1), (1, 0), (1, 1))
STAGES = ((0, 1, 2, 3), (4, 5, 6, 7))
ORDER = (2, 3, 6, 7, 0, 1)
BACK = (0, 1, 3, 2, 5, 4, 7, 6)
CUTOFF = 5.0
R3, R5, R15 = math.sqrt(3.0), math.sqrt(5.0), math.sqrt(15.0)
DEGREES = ((0,), (1, 2, 3), (4, 5, 6, 7, 8))
WIDTH = 256
EDGES = 2048
C = 64


def mm(lhs, rhs):
    return jnp.dot(lhs, rhs, preferred_element_type=F32)


def mm_nt(lhs, rhs):
    return lax.dot_general(lhs, rhs, (((1,), (1,)), ((), ())), preferred_element_type=F32)


def turned(block):
    return block.astype(F32).T.astype(BF16)


def gated(half):
    rise = 1.0 + jnp.tanh(half)
    active = half * rise
    return active, rise + active * (2.0 - rise)


def halved(block):
    return (0.5 * block.astype(F32)).astype(BF16)


def pipeline(steps):
    waiting, running = list(steps), []
    while waiting or running:
        if waiting:
            running.append(waiting.pop(0))
        running = [step for step in running if next(step, "end") != "end"]


def onehot(row, count, first=0):
    ids = lax.broadcasted_iota(jnp.int16, (count, row.shape[1]), 0)
    own = (row - first).astype(jnp.int16)
    return jnp.where(ids == own, jnp.bfloat16(1.0), jnp.bfloat16(0.0))


def down(block):
    return jnp.sum(block, axis=0, keepdims=True)


def part(block, i):
    return block[i * C : (i + 1) * C]


def scaled(block, harm):
    return block if harm is None else block * harm


def harmonics(x, y, z):
    return [
        None, R3 * x, R3 * y, R3 * z,
        R15 * x * y, R15 * y * z, 0.5 * R5 * (3.0 * z * z - 1.0), R15 * x * z, 0.5 * R15 * (x * x - y * y),
    ]


def geometry(vec, centre, slot, mask, geo, dense):
    for i in range(3):
        for b in range(16):
            dense[i, b : b + 1, :] = vec[i : i + 1, b * 128 : (b + 1) * 128]
    real = mask[...] > 0
    vx, vy, vz = [jnp.where(real, dense[i], 1.0) for i in range(3)]
    dist = jnp.sqrt(vx * vx + vy * vy + vz * vz)
    inv = 1.0 / dist
    t = dist / CUTOFF
    angle = math.pi * t
    sin1, cos1 = jnp.sin(angle), jnp.cos(angle)
    scale = math.sqrt(2.0 / CUTOFF)
    sins, coss = [jnp.zeros_like(t), sin1], [jnp.ones_like(t), cos1]
    for n in range(2, 9):
        sins.append(2.0 * cos1 * sins[-1] - sins[-2])
        coss.append(2.0 * cos1 * coss[-1] - coss[-2])
    for n in range(1, 9):
        radial = scale * sins[n] * inv
        geo[0, :, n - 1, :] = radial
        geo[1, :, n - 1, :] = (scale * n * math.pi / CUTOFF * coss[n] - radial) * inv
    t2 = t * t
    t4 = t2 * t2
    t5, t6, t7, t8 = t4 * t, t4 * t2, t4 * t2 * t, t4 * t4
    geo[2, :, 0, :] = vx * inv
    geo[2, :, 1, :] = vy * inv
    geo[2, :, 2, :] = vz * inv
    geo[2, :, 3, :] = inv
    geo[2, :, 4, :] = 1.0 - 28.0 * t6 + 48.0 * t7 - 21.0 * t8
    geo[2, :, 5, :] = (336.0 * t6 - 168.0 * t5 - 168.0 * t7) / CUTOFF
    geo[2, :, 6, :] = jnp.where(real, centre[...], -1).astype(F32)
    geo[2, :, 7, :] = jnp.where(real, slot[...], -1).astype(F32)


def kernel(
    space, grp, span,
    vec_in, feat_in, centre_in, slot_in, mask_in, rows_in, w_radial_in, w_centre_in, w_nbr_in, w_env_in, w_val_in,
    w_mix_in, w_scal_in, w_read_in, w_out_in,
    result_ref, rest_ref,
    vec, feat, centre, slot, mask, send_rows, w_radial, w_centre, w_nbr, wevt, w_mix, w_scal, w_read, w_out,
    outgoing, tab, near, geo, dense, wr, wrhl, wev, wmixt, wreadt, wout, woutf,
    hot_s, far_s, lat_s, actb_s, act_s, slope_s, wv_s, back_s, vbar_s, hbar_s, en_s, env_s, envh_s, fsum, leaving, landed,
    in_sem, send_sem, recv_sem, send_sem2, recv_sem2,
):
    wide = span // 128
    chunks = EDGES // span
    me_s, me_g = lax.axis_index("space"), lax.axis_index("grp")
    peers = [(lax.rem(me_s + a + space, space), lax.rem(me_g + b + grp, grp)) for a, b in OFFSETS]
    barrier = pltpu.get_barrier_semaphore()
    for peer in peers:
        pl.semaphore_signal(barrier, inc=1, device_id=peer, device_id_type=MESH)
    pairs = [
        (feat_in, feat), (w_nbr_in, w_nbr), (rows_in, send_rows), (w_centre_in, w_centre), (vec_in, vec), (centre_in, centre),
        (slot_in, slot), (mask_in, mask), (w_radial_in, w_radial), (w_env_in, wevt.at[0:C]), (w_val_in, wevt.at[C : 2 * C]),
        (w_mix_in, w_mix), (w_scal_in, w_scal), (w_read_in, w_read), (w_out_in, w_out),
    ]
    loads = [pltpu.make_async_copy(a, b, in_sem.at[i]) for i, (a, b) in enumerate(pairs)]
    for load in loads:
        load.start()
    for load in loads[:3]:
        load.wait()
    own = (0.5 * mm(feat[...], w_nbr[...])).T.astype(BF16)
    near[:, 0:WIDTH] = own
    outgoing[...] = mm(own, onehot(send_rows[...], WIDTH)).astype(BF16)
    pl.semaphore_wait(barrier, 8)

    mate = 1 - 2 * lax.rem(me_g, 2)
    steps = ((0, mate), (0, -mate), (-1, 0), (1, 0), (-1, mate), (1, mate), (-1, -mate), (1, -mate))
    partners = [(lax.rem(me_s + a + space, space), lax.rem(me_g + b + grp, grp)) for a, b in steps]
    flat = [3 * (a + 1) + b + 1 for a, b in steps]
    blocks = [f - jnp.where(f > 4, 1, 0) for f in flat]

    def remote(source, target, sends, receives, device):
        return pltpu.make_async_remote_copy(
            src_ref=source, dst_ref=target, send_sem=sends, recv_sem=receives, device_id=device, device_id_type=MESH
        )

    def sent(role):
        return remote(outgoing, tab.at[BACK[role]], send_sem.at[role], recv_sem.at[BACK[role]], partners[role])

    def passed(role):
        return remote(tab.at[role - 2], tab.at[role], send_sem.at[role], recv_sem.at[role], partners[0])

    copies = {role: sent(role) for role in ORDER}
    for role in ORDER:
        copies[role].start()
    for load in loads[3:]:
        load.wait()
    near[:, WIDTH:] = (0.5 * mm(feat[...], w_centre[...])).T.astype(BF16)
    geometry(vec, centre, slot, mask, geo, dense)
    half_radial = 0.5 * w_radial[...]
    high = half_radial.astype(BF16).astype(F32)
    low = half_radial - high
    stacked = jnp.concatenate([high, low, high, jnp.zeros((104, WIDTH), F32)], axis=0)
    wr[...] = stacked.T[:, :32].astype(BF16)
    wrhl[...] = jnp.concatenate([high, low], axis=0).astype(BF16)

    def rows(group, j):
        return jnp.concatenate([geo[group, wide * j + i] for i in range(wide)], axis=1)

    def fields(j):
        block = rows(2, j)
        return [block[i : i + 1] for i in range(8)]

    def index(row):
        return row.astype(jnp.int32)

    for j in range(chunks):
        radial = rows(0, j)
        top = radial.astype(BF16).astype(F32)
        terms = jnp.concatenate([top, top, radial - top, jnp.zeros_like(top)], axis=0).astype(BF16)
        marks = fields(j)
        hot_s[j] = onehot(index(marks[6]), WIDTH)
        hot = jnp.concatenate([onehot(index(marks[7]), WIDTH), hot_s[j]], axis=0)
        act_s[j] = mm(near[...], hot) + mm(wr[...], terms)

    wev[...] = turned(wevt[...])
    w_mix[...] = halved(w_mix[...])
    w_scal[...] = halved(w_scal[...])
    w_read[...] = halved(w_read[...])
    wmixt[:, 0:WIDTH] = turned(w_mix[...])
    padded = jnp.concatenate([w_scal[...].astype(F32), jnp.zeros((C, WIDTH), F32)], axis=0)
    wmixt[:, WIDTH:] = padded.T.astype(BF16)
    wreadt[...] = turned(w_read[...])
    woutf[...] = jnp.broadcast_to(w_out[...], (128, WIDTH)).T
    wout[...] = woutf[...].astype(BF16)
    for j in range(chunks):
        slots = index(fields(j)[7])
        far_s[j] = jnp.concatenate([onehot(slots, 128, WIDTH + 128 * c) for c in blocks], axis=0)

    def add(total, term, j):
        total[...] = term if j == 0 else total[...] + term

    def gathered(j, stage):
        hot = far_s[j, 128 * stage[0] : 128 * (stage[-1] + 1)]
        return act_s[j] + mm(jnp.concatenate([tab[role] for role in stage], axis=1), hot)

    for role in (2, 3):
        copies[BACK[role]].wait_recv()
        copies[role + 2] = passed(role + 2)
        copies[role + 2].start()
    for role in (0, 1):
        copies[role].wait_recv()
    for j in range(chunks):
        act_s[j] = gathered(j, STAGES[0])
    for role in (4, 5):
        copies[role].wait_recv()
    for role in (6, 7):
        copies[BACK[role]].wait_recv()

    def forward(j):
        x, y, z, _, envelope, _, _, _ = fields(j)
        lifted = gathered(j, STAGES[1])
        yield
        active, slope = gated(lifted)
        actb_s[j] = active.astype(BF16)
        slope_s[j] = slope
        latent = (active * envelope).astype(BF16)
        lat_s[j, 0:WIDTH] = latent
        yield
        wv = mm(wevt[...], latent)
        wv_s[j] = wv
        yield
        weights = wv[:C]
        harm = harmonics(x, y, z)
        spread = jnp.concatenate([scaled(weights, harm[i]).astype(BF16) for i in range(9)], axis=0)
        yield
        add(env_s, mm_nt(spread, hot_s[j]), j)

    def middle(j):
        x, y, z, _, _, _, _, _ = fields(j)
        hot = hot_s[j]
        harm = harmonics(x, y, z)
        local = mm(envh_s[...], hot)
        yield
        values = wv_s[j, C:]
        invariants = []
        for degree in DEGREES:
            whole = None
            for i in degree:
                term = scaled(part(local, i), harm[i])
                whole = term if whole is None else whole + term
            invariants.append(whole)
        lat_s[j, WIDTH:] = jnp.concatenate([(q * values).astype(BF16) for q in invariants] + [jnp.zeros((C, span), BF16)], axis=0)
        yield
        update = mm(wmixt[...], lat_s[j])
        yield
        active, slope = gated(update)
        mixed = (lat_s[j, 0:WIDTH].astype(F32) + active).astype(BF16)
        yield
        hidden = mm(wreadt[...], mixed)
        yield
        active_h, slope_h = gated(hidden)
        en_s[j] = down(active_h * jnp.concatenate([woutf[...]] * wide, axis=1))
        hidden_bar = jnp.concatenate([wout[...]] * wide, axis=1) * slope_h.astype(BF16)
        yield
        mixed_bar = mm(w_read[...], hidden_bar)
        yield
        mixed_bar = mixed_bar.astype(BF16)
        update_bar = mixed_bar * slope.astype(BF16)
        yield
        back_s[j] = mixed_bar.astype(F32) + mm(w_mix[...], update_bar)
        scal_bar = mm(w_scal[...], update_bar)
        yield
        values_bar = None
        locals_bar, products = [], []
        for level, degree in enumerate(DEGREES):
            bar = part(scal_bar, level)
            term = bar * invariants[level]
            values_bar = term if values_bar is None else values_bar + term
            inner = bar * values
            for i in degree:
                locals_bar.append(scaled(inner, harm[i]).astype(BF16))
                if i:
                    products.append(down(part(local, i) * inner))
        vbar_s[j] = values_bar.astype(BF16)
        hbar_s[j] = jnp.concatenate(products, axis=0)
        yield
        add(env_s, mm_nt(jnp.concatenate(locals_bar, axis=0), hot), j)

    def backward(j):
        x, y, z, inv, envelope, slope_env, centres, slots = fields(j)
        slots, centres = index(slots), index(centres)
        hot = hot_s[j]
        harm = harmonics(x, y, z)
        spread_bar = mm(envh_s[...], hot)
        yield
        weights = wv_s[j, :C]
        weights_bar = part(spread_bar, 0)
        for i in range(1, 9):
            weights_bar = weights_bar + part(spread_bar, i) * harm[i]
        products = [down(part(spread_bar, i) * weights) for i in range(1, 9)]
        wv_bar = jnp.concatenate([weights_bar.astype(BF16), vbar_s[j]], axis=0)
        yield
        latent_bar = back_s[j] + mm(wev[...], wv_bar)
        harm_bar = hbar_s[j] + jnp.concatenate(products, axis=0)
        bars = [None] + [harm_bar[i : i + 1] for i in range(8)]
        yield
        envelope_bar = down(latent_bar * actb_s[j].astype(F32))
        lifted_bar = (latent_bar * envelope * slope_s[j]).astype(BF16)
        yield
        radial_bar = mm(wrhl[...], lifted_bar)
        yield
        dist_bar = down((radial_bar[:8] + radial_bar[8:]) * rows(1, j)) + envelope_bar * slope_env
        ux = R3 * bars[1] + R15 * (y * bars[4] + z * bars[7] + x * bars[8])
        uy = R3 * bars[2] + R15 * (x * bars[4] + z * bars[5] - y * bars[8])
        uz = R3 * bars[3] + R15 * (y * bars[5] + x * bars[7]) + 3.0 * R5 * z * bars[6]
        along = dist_bar - (x * ux + y * uy + z * uz) * inv
        grads = jnp.concatenate([ux * inv + x * along, uy * inv + y * along, uz * inv + z * along, en_s[j]], axis=0)
        top = grads.astype(BF16).astype(F32)
        both = jnp.concatenate([top, grads - top], axis=0)
        split = [jnp.where(lax.shift_right_arithmetic(slots, 7) == h, both, 0.0) for h in range(10)]
        split += [jnp.where(lax.shift_right_arithmetic(centres, 7) == h, both, 0.0) for h in range(2)]
        low = jnp.concatenate([onehot(lax.bitwise_and(row, 127), 128) for row in (slots, centres)], axis=0)
        yield
        add(fsum, mm_nt(jnp.concatenate(split, axis=0).astype(BF16), low), j)

    pipeline(forward(j) for j in range(chunks))
    envh_s[...] = (env_s[...] * 0.125).astype(BF16)
    pipeline(middle(j) for j in range(chunks))
    envh_s[...] = (env_s[...] * 0.125).astype(BF16)
    pipeline(backward(j) for j in range(chunks))

    def summed(first, side):
        return fsum[first : first + 4, 128 * side : 128 * side + 128] + fsum[first + 4 : first + 8, 128 * side : 128 * side + 128]

    for c in range(8):
        leaving[c, 0:4] = summed(16 + 8 * c, 0)
        leaving[c, 4:8] = jnp.zeros((4, 128), F32)
    returns = [remote(leaving.at[c], landed.at[7 - c], send_sem2.at[c], recv_sem2.at[7 - c], peers[c]) for c in range(8)]
    for c in (0, 2, 5, 7, 1, 6, 3, 4):
        returns[c].start()
    centre_sum = jnp.concatenate([summed(80, 1), summed(88, 1)], axis=1)
    own_sum = jnp.concatenate([summed(0, 0), summed(8, 0)], axis=1)
    hot = onehot(send_rows[...], WIDTH)
    for copy in returns:
        copy.wait_recv()
    total = landed[0]
    for c in range(1, 8):
        total = total + landed[c]
    top = total.astype(BF16).astype(F32)
    away = mm_nt(jnp.concatenate([top, total - top], axis=0).astype(BF16), hot)
    result_ref[...] = centre_sum
    rest_ref[0:3] = -own_sum[0:3] - (away[0:3] + away[8:11])
    rest_ref[3:4] = jnp.zeros((1, WIDTH), F32)
    for copy in list(copies.values()) + returns:
        copy.wait_send()


def per_device(
    space, grp,
    rel_vec, atom_feat, centre, nbr_slot, edge_mask, send_rows, w_radial, w_centre, w_nbr, w_env, w_val, w_mix, w_scal,
    w_read, w_out,
):
    span = 512
    chunks = EDGES // span
    shape = jax.ShapeDtypeStruct
    vm = pltpu.VMEM
    result = pl.pallas_call(
        functools.partial(kernel, space, grp, span),
        out_shape=[vm((4, WIDTH), F32)] * 2,
        in_specs=[pl.BlockSpec(memory_space=pl.ANY)] * 15,
        out_specs=[pl.BlockSpec(memory_space=pltpu.VMEM)] * 2,
        scratch_shapes=[
            vm((3, EDGES), F32), vm((WIDTH, WIDTH), BF16), vm((16, 128), jnp.int32), vm((16, 128), jnp.int32),
            vm((16, 128), jnp.int32), vm((1, 128), jnp.int32), vm((8, WIDTH), F32), vm((WIDTH, WIDTH), BF16),
            vm((WIDTH, WIDTH), BF16), vm((2 * C, WIDTH), BF16), vm((WIDTH, WIDTH), BF16), vm((3 * C, WIDTH), BF16),
            vm((WIDTH, WIDTH), BF16), vm((1, WIDTH), F32),
            vm((WIDTH, 128), BF16), vm((8, WIDTH, 128), BF16), vm((WIDTH, 2 * WIDTH), BF16), vm((3, 16, 8, 128), F32),
            vm((3, 16, 128), F32), vm((WIDTH, 32), BF16), vm((16, WIDTH), BF16), vm((WIDTH, 2 * C), BF16),
            vm((WIDTH, 2 * WIDTH), BF16), vm((WIDTH, WIDTH), BF16), vm((WIDTH, 128), BF16), vm((WIDTH, 128), F32),
            vm((chunks, WIDTH, span), BF16), vm((chunks, 8 * 128, span), BF16),
            vm((chunks, 2 * WIDTH, span), BF16), vm((chunks, WIDTH, span), BF16), vm((chunks, WIDTH, span), F32),
            vm((chunks, WIDTH, span), F32), vm((chunks, 2 * C, span), F32), vm((chunks, WIDTH, span), F32),
            vm((chunks, C, span), BF16), vm((chunks, 8, span), F32), vm((chunks, 1, span), F32), vm((9 * C, WIDTH), F32),
            vm((9 * C, WIDTH), BF16),
            vm((96, WIDTH), F32), vm((8, 8, 128), F32), vm((8, 8, 128), F32),
            pltpu.SemaphoreType.DMA((15,)), pltpu.SemaphoreType.DMA((8,)), pltpu.SemaphoreType.DMA((8,)),
            pltpu.SemaphoreType.DMA((8,)), pltpu.SemaphoreType.DMA((8,)),
        ],
        compiler_params=pltpu.CompilerParams(collective_id=0, has_side_effects=True, vmem_limit_bytes=56 * 1024 * 1024),
        name="layer",
    )(
        rel_vec, atom_feat, centre.reshape(16, 128), nbr_slot.reshape(16, 128), edge_mask.reshape(16, 128), send_rows, w_radial,
        w_centre, w_nbr, w_env.T, w_val.T, w_mix, w_scal, w_read, w_out.reshape(1, WIDTH),
    )
    total = result[0] + result[1]
    return (total[3], total[0:3])


def solution(mesh):
    edges = P(("space", "grp"))
    placed = (
        P(None, ("space", "grp")), P(("space", "grp"), None), edges, edges, edges, P(("space", "grp"), None),
    ) + (P(),) * 9
    return jax.shard_map(
        functools.partial(per_device, mesh.shape["space"], mesh.shape["grp"]),
        mesh=mesh,
        in_specs=placed,
        out_specs=(edges, P(None, ("space", "grp"))),
        check_vma=False,
    )
```
